256 devices in a mesh: chan: 32 (over y, x, core), win: 8 (over z).
Axes of the slice: x: 4, y: 4, z: 8, core: 2. Of those that a mesh axis runs over, the one named last changes fastest.
Arguments:
- traces: bfloat16 [48, 8192, 1024], P('win', 'chan'), may hold values from -200 to 200
- offsets: int32 [32, 3], replicated, may hold values from -3 to 3, as said below
- counts: int32 [32], replicated, may hold values from 1 to 3, as said below
Outputs:
- correlations: float32 [96, 256, 1024], P('chan', 'win')
The draws below stay inside these ranges and needn't reach their ends.
Inputs may be any that keep to these rules, and one draw needn't show every extreme that they name: Each row o holds 3 distinct nonzero offsets, and o + offsets[o, p] names a block, 0 to 31. `counts`: at least one owner has all 3 slots live.
All inputs are finite; a program needn't handle non-finite values.
Results may differ from the reference program's by a relative error of at most 0.0052.
Values may be sent and summed in bfloat16 or wider, within the bound.
A program may use at most 128 MiB of HBM per device.

```python
import math
import jax
import jax.numpy as jnp
from jax import lax

NT = 1024
NF = 512
BLOCK = 256
RADIUS = 8
MAXOFF = 3
PAIRS_DEV = 3
BLOCKS = 32
CHANNELS = 8192
SEGS = 48


def draw_traces(key, part):
    key = jax.random.fold_in(key, 13)
    noise_key, channel_key, segment_key = jax.random.split(key, 3)
    channel_scale = jnp.exp(jax.random.uniform(channel_key, (1, CHANNELS, 1), jnp.float32) * math.log(10.0))
    segment_scale = jnp.exp(jax.random.uniform(segment_key, (SEGS, 1, 1), jnp.float32) * math.log(3.0))
    samples_noise = jax.random.normal(noise_key, (SEGS, CHANNELS, NT), jnp.float32)
    values = samples_noise * channel_scale * segment_scale
    return jnp.clip(values, -200.0, 200.0).astype(jnp.bfloat16)


def draw_offsets(key, part):
    key = jax.random.fold_in(key, 11)
    candidates = jnp.concatenate([jnp.arange(-MAXOFF, 0, dtype=jnp.int32), jnp.arange(1, MAXOFF + 1, dtype=jnp.int32)])
    owner_index = jnp.arange(BLOCKS, dtype=jnp.int32)[:, None]
    target = owner_index + candidates[None, :]
    allowed = (target >= 0) & (target < BLOCKS)
    scores = jax.random.randint(key, (BLOCKS, 2 * MAXOFF), 0, 1 << 20) * (2 * MAXOFF) + jnp.arange(2 * MAXOFF, dtype=jnp.int32)[None, :]
    scores = jnp.where(allowed, scores + (1 << 26), scores)
    leading = (candidates[None, :] == -owner_index) & (owner_index >= 1) & (owner_index <= MAXOFF)
    scores = jnp.where(leading, scores + (1 << 27), scores)
    chosen = lax.top_k(scores, PAIRS_DEV)[1]
    return candidates[chosen].astype(jnp.int32)


def draw_counts(key, part):
    key = jax.random.fold_in(key, 12)
    level_key, owner_key = jax.random.split(key)
    rolls = jax.random.randint(level_key, (BLOCKS,), 0, 4)
    live_count = jnp.where(rolls == 0, PAIRS_DEV, 1)
    busiest = jax.random.randint(owner_key, (), 0, BLOCKS)
    owner_index = jnp.arange(BLOCKS, dtype=jnp.int32)
    live_count = jnp.where(owner_index == busiest, PAIRS_DEV, live_count)
    live_count = jnp.where(owner_index == 0, PAIRS_DEV, live_count)
    return live_count.astype(jnp.int32)


def setup_inputs(seed: int = 0) -> dict:
    streams_of = jax.random.split(jax.random.key(seed), 4)
    return {
        "traces": draw_traces(jax.random.fold_in(streams_of[3], 71), 0),
        "offsets": draw_offsets(jax.random.fold_in(streams_of[3], 71), 0),
        "counts": draw_counts(jax.random.fold_in(streams_of[3], 71), 0),
    }


WATER = 0.8
EPS = 1e-06

def forward_table():
    column = jnp.arange(2 * NF, dtype=jnp.int32)
    frequency = column % NF
    part_im = column // NF
    samples_axis = jnp.arange(NT, dtype=jnp.int32)
    phase_index = samples_axis[:, None] * frequency[None, :] % NT
    angles = phase_index.astype(jnp.float32) * (2.0 * math.pi / NT)
    return jnp.where(part_im[None, :] == 0, jnp.cos(angles), -jnp.sin(angles)).astype(jnp.bfloat16)

def inverse_table():
    column = jnp.arange(2 * NF, dtype=jnp.int32)
    frequency = column % NF
    part_im = column // NF
    samples_axis = jnp.arange(NT, dtype=jnp.int32)
    phase_index = frequency[:, None] * samples_axis[None, :] % NT
    angles = phase_index.astype(jnp.float32) * (2.0 * math.pi / NT)
    return jnp.where(part_im[:, None] == 0, jnp.cos(angles), -jnp.sin(angles))

def whiten_rows(spectra):
    real_part = spectra[:, :NF]
    imag_part = spectra[:, NF:]
    amplitude = jnp.sqrt(real_part * real_part + imag_part * imag_part)
    windowed = lax.reduce_window(amplitude, jnp.zeros((), amplitude.dtype), lax.add, (1, 2 * RADIUS + 1), (1, 1), ((0, 0), (RADIUS, RADIUS)))
    frequency = jnp.arange(NF, dtype=jnp.int32)
    bin_count = (jnp.minimum(frequency + RADIUS, NF - 1) - jnp.maximum(frequency - RADIUS, 0) + 1).astype(amplitude.dtype)
    smooth = windowed / bin_count[None, :]
    water_level = WATER * lax.optimization_barrier(jnp.mean(amplitude, axis=1, keepdims=True)) + EPS
    divisor = jnp.maximum(smooth, water_level)
    return jnp.concatenate([real_part / divisor, imag_part / divisor], axis=1).astype(jnp.bfloat16)

def reference(traces, offsets, counts):
    dft_table = forward_table()

    def one_segment(segment):
        spectra = jnp.dot(segment, dft_table, preferred_element_type=jnp.float32)
        return whiten_rows(spectra)
    whitened = lax.map(one_segment, traces)
    blocks = whitened.reshape(SEGS, BLOCKS, BLOCK, 2 * NF)
    inverse = inverse_table()
    norm_factor = 1.0 / math.sqrt(NF * SEGS)

    def one_owner(owner_index):
        source = lax.dynamic_index_in_dim(blocks, owner_index, 1, keepdims=False).astype(jnp.float32)
        source_real = source[:, :, :NF]
        source_imag = source[:, :, NF:]
        pair_rows = []
        for slot_index in range(PAIRS_DEV):
            target = (owner_index + offsets[owner_index, slot_index]).astype(jnp.int32)
            receiver = lax.dynamic_index_in_dim(blocks, target, 1, keepdims=False).astype(jnp.float32)
            receiver_real = receiver[:, :, :NF]
            receiver_imag = receiver[:, :, NF:]
            real_sum = lax.optimization_barrier(jnp.sum(source_real * receiver_real + source_imag * receiver_imag, axis=0))
            imag_sum = lax.optimization_barrier(jnp.sum(source_real * receiver_imag - source_imag * receiver_real, axis=0))
            cross_spec = jnp.concatenate([real_sum, imag_sum], axis=1)
            active = slot_index < counts[owner_index]
            cross_spec = jnp.where(active, cross_spec, jnp.zeros_like(cross_spec))
            pair_rows.append(jnp.dot(cross_spec, inverse, precision=lax.Precision.HIGHEST, preferred_element_type=jnp.float32) * norm_factor)
        return jnp.stack(pair_rows)
    result = lax.map(one_owner, jnp.arange(BLOCKS, dtype=jnp.int32))
    return result.reshape(BLOCKS * PAIRS_DEV, BLOCK, NT)
```

```python
import functools
import math

import jax
import jax.numpy as jnp
import numpy as np
from jax import lax
from jax.experimental import pallas as pl
from jax.experimental.pallas import tpu as pltpu
from jax.sharding import PartitionSpec as P

MESH = pl.DeviceIdType.MESH
RADIUS = 8
HALO = 3
SLOTS = 3
WATER = 0.8
EPS = 1e-06
ROW = 8
WIN = 8
HALF = 16
LANES = 128


def forward_table(length):
    column = np.arange(length)
    phase = np.arange(length)[:, None] * (column % (length // 2))[None, :] % length
    angles = phase * (2.0 * math.pi / length)
    table = np.where(column[None, :] < length // 2, np.cos(angles), -np.sin(angles))
    return table.astype(jnp.bfloat16)


def inverse_table(length):
    column = np.arange(length)
    phase = np.arange(length)[None, :] * (column % (length // 2))[:, None] % length
    angles = phase * (2.0 * math.pi / length)
    table = np.where(column[:, None] < length // 2, np.cos(angles), -np.sin(angles))
    return table.astype(jnp.bfloat16)


def band_table(bins):
    place = np.arange(bins)
    return (np.abs(place[:, None] - place[None, :]) <= RADIUS).astype(jnp.bfloat16)


def window_weight(bins):
    place = np.arange(bins)
    count = np.minimum(place + RADIUS, bins - 1) - np.maximum(place - RADIUS, 0) + 1
    return np.broadcast_to((1.0 / count).astype(np.float32), (8, bins))


def kernel(
    norm, offsets, counts, traces, forward, band, inverse, weight, out,
    tr, fwd, bnd, inv, spec, high, low, smooth, water, white, got, near, part, zout, zin, fout, fin, left,
    tab_sem, tr_sem, xs, xr, ys, yr, zs, zr, fs, fr,
):
    segments, bins = tr.shape[1], bnd.shape[0]
    groups = bins // LANES
    chan, win = lax.axis_index("chan"), lax.axis_index("win")
    row, place = chan // ROW, chan % ROW
    first = row * ROW
    above = lax.rem(row + 1, 4) * ROW + place
    below = lax.rem(row + 3, 4) * ROW + place
    after, before = lax.rem(win + 1, WIN), lax.rem(win + WIN - 1, WIN)

    barrier = pltpu.get_barrier_semaphore()
    mates = [(first + lax.rem(place + k, ROW), win) for k in range(1, ROW)]
    partners = mates + [(above, win), (below, win), (chan, after), (chan, before)]
    for partner in partners:
        pl.semaphore_signal(barrier, inc=1, device_id=partner, device_id_type=MESH)

    def chunk_of(t):
        half = 4 - (t + 1) // 2
        return lax.rem(win + jnp.where(t % 2 == 1, WIN - half, half), WIN)

    def trace_copy(t):
        rows = pl.ds(pl.multiple_of(chunk_of(t) * 2 * HALF, 2 * HALF), 2 * HALF)
        return pltpu.make_async_copy(traces.at[:, rows, :], tr.at[t], tr_sem.at[t])

    tables = [
        pltpu.make_async_copy(forward, fwd, tab_sem.at[0]),
        pltpu.make_async_copy(band, bnd, tab_sem.at[1]),
        pltpu.make_async_copy(inverse, inv, tab_sem.at[2]),
    ]
    tables[0].start()
    trace_copy(0).start()
    tables[1].start()

    def start_traces(t, carry):
        trace_copy(t).start()
        return carry

    lax.fori_loop(1, WIN, start_traces, 0)
    tables[2].start()
    tables[0].wait()
    tables[1].wait()

    def whiten(t):
        trace_copy(t).wait()
        lhs = tr[t].reshape(segments * 2 * HALF, 2 * bins)
        spec[...] = jnp.dot(lhs, fwd[...], preferred_element_type=jnp.float32)

        def amplitudes(i, carry):
            rows = pl.ds(pl.multiple_of(i * HALF, HALF), HALF)
            re, im = spec[rows, :bins], spec[rows, bins:]
            amp = jnp.sqrt(re * re + im * im)
            top = amp.astype(jnp.bfloat16)
            high[rows, :] = top
            low[rows, :] = (amp - top.astype(jnp.float32)).astype(jnp.bfloat16)
            mean = jnp.sum(amp, axis=1, keepdims=True) * (1.0 / bins)
            water[rows, :] = jnp.broadcast_to(WATER * mean + EPS, (HALF, LANES))
            return carry

        lax.fori_loop(0, 2 * segments, amplitudes, 0)
        smooth[...] = jnp.dot(high[...], bnd[...], preferred_element_type=jnp.float32) + jnp.dot(
            low[...], bnd[...], preferred_element_type=jnp.float32
        )

        def divide(s, carry):
            for h in range(2):
                rows = pl.ds(pl.multiple_of(s * 2 * HALF + h * HALF, HALF), HALF)
                level = water[rows, :]
                for g in range(groups):
                    lanes = slice(g * LANES, (g + 1) * LANES)
                    scale = 1.0 / jnp.maximum(smooth[rows, lanes] * weight[0:1, lanes], level)
                    re = spec[rows, lanes] * scale
                    im = spec[rows, slice(bins + g * LANES, bins + (g + 1) * LANES)] * scale
                    white[t, 2 * g + h, 0, s] = re.astype(jnp.bfloat16)
                    white[t, 2 * g + h, 1, s] = im.astype(jnp.bfloat16)
            return carry

        lax.fori_loop(0, segments, divide, 0)

    def send_row(t):
        for k, mate in enumerate(mates):
            other = lax.rem(place + k + 1, ROW)
            pltpu.make_async_remote_copy(
                white.at[t, other], got.at[t, HALO + place], xs.at[t], xr.at[t], device_id=mate, device_id_type=MESH
            ).start()
        got[t, HALO + place] = white[t, place]

    def row_wait(t):
        block = got.at[t, pl.ds(0, ROW - 1)]
        return pltpu.make_async_remote_copy(block, block, xs.at[t], xr.at[t], device_id=mates[0], device_id_type=MESH)

    def near_copy(t, source, target, device):
        return pltpu.make_async_remote_copy(
            got.at[t, pl.ds(source, HALO)],
            got.at[t, pl.ds(target, HALO)],
            ys.at[t],
            yr.at[t],
            device_id=(device, win),
            device_id_type=MESH,
        )

    def near_wait(t):
        block = got.at[t, pl.ds(0, 2 * HALO)]
        return pltpu.make_async_remote_copy(
            block, block, ys.at[t], yr.at[t], device_id=(above, win), device_id_type=MESH
        )

    def chain_copy(t):
        target = jnp.where((t % 2 == 0) & (t > 0), after, before)
        return pltpu.make_async_remote_copy(
            zout.at[t], zin.at[t], zs.at[t], zr.at[t], device_id=(chan, target), device_id_type=MESH
        )

    def cross(t):
        def move(b, carry):
            near[b] = got[t, b]
            return carry

        lax.fori_loop(0, ROW + 2 * HALO, move, 0)

        def owner(j, carry):
            source = [
                (near[HALO + j, 0, s].astype(jnp.float32), near[HALO + j, 1, s].astype(jnp.float32))
                for s in range(segments)
            ]
            for p in range(SLOTS):
                receiver = HALO + j + offsets[first + j, p]
                live = p < counts[first + j]
                total_re = jnp.zeros((HALF, LANES), jnp.float32)
                total_im = jnp.zeros((HALF, LANES), jnp.float32)
                for s, (ar, ai) in enumerate(source):
                    br = near[receiver, 0, s].astype(jnp.float32)
                    bi = near[receiver, 1, s].astype(jnp.float32)
                    total_re += ar * br + ai * bi
                    total_im += ar * bi - ai * br
                part[SLOTS * j + p, 0] = jnp.where(live, total_re, 0.0)
                part[SLOTS * j + p, 1] = jnp.where(live, total_im, 0.0)
            return carry

        lax.fori_loop(0, ROW, owner, 0)

    def add_up(t):
        @pl.when((t == 1) | (t > 2))
        def _():
            slot = jnp.where(t == 1, 0, jnp.maximum(t - 2, 0))
            chain_copy(slot).wait_recv()

            def add(q, carry):
                part[q] = part[q] + zin[slot, q].astype(jnp.float32)
                return carry

            lax.fori_loop(0, SLOTS * ROW, add, 0)

        @pl.when(t < WIN - 1)
        def _():
            def store(q, carry):
                zout[t, q] = part[q].astype(jnp.bfloat16)
                return carry

            lax.fori_loop(0, SLOTS * ROW, store, 0)
            chain_copy(t).start()

    def forward_step(t, carry):
        whiten(t)

        @pl.when(t == 0)
        def _():
            pl.semaphore_wait(barrier, len(partners))

        send_row(t)
        return carry

    lax.fori_loop(0, WIN, forward_step, 0)

    def pair_step(t, carry):
        @pl.when(t < WIN)
        def _():
            row_wait(t).wait_recv()
            near_copy(t, HALO, HALO + ROW, below).start()
            near_copy(t, ROW, 0, above).start()

        @pl.when(t > 0)
        def _():
            near_wait(t - 1).wait_recv()
            cross(t - 1)
            add_up(t - 1)

        return carry

    lax.fori_loop(0, WIN + 1, pair_step, 0)

    last = WIN - 2
    chain_copy(last).wait_recv()

    def finish(q, carry):
        fout[q] = (part[q] + zin[last, q].astype(jnp.float32)).astype(jnp.bfloat16)
        return carry

    lax.fori_loop(0, SLOTS * ROW, finish, 0)
    for k, mate in enumerate(mates):
        other = lax.rem(place + k + 1, ROW)
        pltpu.make_async_remote_copy(
            fout.at[pl.ds(SLOTS * other, SLOTS)], fin.at[place], fs, fr, device_id=mate, device_id_type=MESH
        ).start()
    fin[place] = fout[pl.ds(SLOTS * place, SLOTS)]
    tables[2].wait()
    final = fin.at[pl.ds(0, ROW - 1)]
    final_wait = pltpu.make_async_remote_copy(final, final, fs, fr, device_id=mates[0], device_id_type=MESH)
    final_wait.wait_recv()
    for g in range(groups):
        for h in range(2):
            for p in range(SLOTS):
                rows = slice((2 * p + h) * HALF, (2 * p + h + 1) * HALF)
                left[rows, g * LANES : (g + 1) * LANES] = fin[2 * g + h, p, 0]
                left[rows, bins + g * LANES : bins + (g + 1) * LANES] = fin[2 * g + h, p, 1]
    result = jnp.dot(left[...], inv[...], preferred_element_type=jnp.float32) * norm
    out[...] = result.reshape(out.shape)

    final_wait.wait_send()

    def drain(t, carry):
        row_wait(t).wait_send()
        near_wait(t).wait_send()

        @pl.when(t < WIN - 1)
        def _():
            chain_copy(t).wait_send()

        return carry

    lax.fori_loop(0, WIN, drain, 0)


def body(traces, offsets, counts):
    segments, channels, length = traces.shape
    bins = length // 2
    norm = 1.0 / math.sqrt(bins * segments * WIN)
    rows = segments * 2 * HALF
    bf16, f32 = jnp.bfloat16, jnp.float32
    pairs = SLOTS * ROW
    share = (2, HALF, LANES)
    block = (2, segments, HALF, LANES)
    any_space, vmem, smem = (pl.BlockSpec(memory_space=s) for s in (pl.ANY, pltpu.VMEM, pltpu.SMEM))
    dma = pltpu.SemaphoreType.DMA
    return pl.pallas_call(
        functools.partial(kernel, norm),
        out_shape=jax.ShapeDtypeStruct((SLOTS, channels // WIN, length), f32),
        in_specs=[smem, smem, any_space, any_space, any_space, any_space, vmem],
        out_specs=vmem,
        scratch_shapes=[
            pltpu.VMEM((WIN, segments, 2 * HALF, length), bf16),
            pltpu.VMEM((length, length), bf16),
            pltpu.VMEM((bins, bins), bf16),
            pltpu.VMEM((length, length), bf16),
            pltpu.VMEM((rows, length), f32),
            pltpu.VMEM((rows, bins), bf16),
            pltpu.VMEM((rows, bins), bf16),
            pltpu.VMEM((rows, bins), f32),
            pltpu.VMEM((rows, LANES), f32),
            pltpu.VMEM((WIN, ROW) + block, bf16),
            pltpu.VMEM((WIN, ROW + 2 * HALO) + block, bf16),
            pltpu.VMEM((ROW + 2 * HALO,) + block, bf16),
            pltpu.VMEM((pairs,) + share, f32),
            pltpu.VMEM((WIN - 1, pairs) + share, bf16),
            pltpu.VMEM((WIN - 1, pairs) + share, bf16),
            pltpu.VMEM((pairs,) + share, bf16),
            pltpu.VMEM((ROW, SLOTS) + share, bf16),
            pltpu.VMEM((SLOTS * 2 * HALF, length), bf16),
            dma((3,)),
            dma((WIN,)),
            dma((WIN,)),
            dma((WIN,)),
            dma((WIN,)),
            dma((WIN,)),
            dma((WIN - 1,)),
            dma((WIN - 1,)),
            dma,
            dma,
        ],
        compiler_params=pltpu.CompilerParams(collective_id=0, has_side_effects=True, vmem_limit_bytes=48 << 20),
    )(
        offsets,
        counts,
        traces,
        jnp.asarray(forward_table(length)),
        jnp.asarray(band_table(bins)),
        jnp.asarray(inverse_table(length)),
        jnp.asarray(window_weight(bins)),
    )


def solution(mesh):
    in_specs = (P("win", "chan", None), P(), P())
    out_specs = P("chan", "win", None)
    return jax.shard_map(body, mesh=mesh, in_specs=in_specs, out_specs=out_specs, check_vma=False)
```

```python
import functools
import math

import jax
import jax.numpy as jnp
import numpy as np
from jax import lax
from jax.experimental import pallas as pl
from jax.experimental.pallas import tpu as pltpu
from jax.sharding import PartitionSpec as P

MESH = pl.DeviceIdType.MESH
RADIUS = 8
HALO = 3
SLOTS = 3
WATER = 0.8
EPS = 1e-06
ROW = 8
WIN = 8
PART = 16
SHARE = 8
LANES = 128
VMEM_BYTES = 62 << 20

ORDER = [(-4, 0), (-4, 1), (-3, 0), (-3, 1), (3, 0), (3, 1), (-2, 0), (-2, 1), (2, 0), (2, 1)]
ORDER += [(-1, 0), (1, 0), (-1, 1), (1, 1), (0, 0), (0, 1)]
STEPS = len(ORDER)
OUTSIDE = STEPS - 2
AHEAD = 3
BEHIND = 5


def forward_table(length):
    column = np.arange(length)
    phase = np.arange(length)[:, None] * (column % (length // 2))[None, :] % length
    angles = phase * (2.0 * math.pi / length)
    table = np.where(column[None, :] < length // 2, np.cos(angles), -np.sin(angles))
    return table.astype(jnp.bfloat16)


def inverse_table(length):
    column = np.arange(length)
    phase = np.arange(length)[None, :] * (column % (length // 2))[:, None] % length
    angles = phase * (2.0 * math.pi / length)
    table = np.where(column[:, None] < length // 2, np.cos(angles), -np.sin(angles))
    return table.astype(jnp.bfloat16)


def band_table(bins):
    place = np.arange(bins)
    return (np.abs(place[:, None] - place[None, :]) <= RADIUS).astype(jnp.bfloat16)


def arrival(step):
    where, half = ORDER[step]
    if where in (-4, 3):
        return -1
    return ORDER.index((where - 1 if where <= 0 else where + 1, half))


def look_up(step, values):
    found = jnp.int32(values[0])
    for k, value in enumerate(values[1:], 1):
        if value != values[0]:
            found = jnp.where(step == k, jnp.int32(value), found)
    return found


def kernel(
    norm, offsets_in, counts_in, traces, forward, band, inverse, out,
    offsets, counts, tr, fwd, bnd, inv, weight, spec, high, low, smooth, water, white, got, near, part, zout, zin,
    fout, fin, left, tab_sem, tr_sem, xs, xr, ys, yr, zs, zr, fs, fr,
):
    segments, bins = tr.shape[1], bnd.shape[0]
    groups = bins // LANES
    chan, win = lax.axis_index("chan"), lax.axis_index("win")
    row, place = chan // ROW, chan % ROW
    first = row * ROW
    above = lax.rem(row + 1, 4) * ROW + place
    below = lax.rem(row + 3, 4) * ROW + place
    after, before = lax.rem(win + 1, WIN), lax.rem(win + WIN - 1, WIN)

    barrier = pltpu.get_barrier_semaphore()
    mates = [(first + lax.rem(place + k, ROW), win) for k in range(1, ROW)]
    partners = mates + [(above, win), (below, win), (chan, after), (chan, before)]
    for partner in partners:
        pl.semaphore_signal(barrier, inc=1, device_id=partner, device_id_type=MESH)

    def trace_copy(i):
        target = lax.rem(win + look_up(i, [(where + WIN) % WIN for where, _ in ORDER]), WIN)
        half = look_up(i, [half for _, half in ORDER])
        rows = pl.ds(pl.multiple_of((2 * target + half) * PART, PART), PART)
        return pltpu.make_async_copy(traces.at[:, rows, :], tr.at[i], tr_sem.at[i])

    tables = [
        pltpu.make_async_copy(source, target, tab_sem.at[k])
        for k, (source, target) in enumerate(
            [(forward, fwd), (band, bnd), (inverse, inv), (offsets_in, offsets), (counts_in, counts)]
        )
    ]
    tables[0].start()
    trace_copy(0).start()
    tables[1].start()

    def start_traces(i, carry):
        trace_copy(i).start()
        return carry

    lax.fori_loop(1, STEPS, start_traces, 0)
    for table in tables[2:]:
        table.start()
    bin_of = lax.broadcasted_iota(jnp.int32, weight.shape, 1)
    count = jnp.minimum(bin_of + RADIUS, bins - 1) - jnp.maximum(bin_of - RADIUS, 0) + 1
    weight[...] = 1.0 / count.astype(jnp.float32)
    tables[0].wait()
    tables[1].wait()

    def whiten(i):
        trace_copy(i).wait()
        lhs = tr[i].reshape(segments * PART, 2 * bins)
        spec[...] = jnp.dot(lhs, fwd[...], preferred_element_type=jnp.float32)
        for s in range(segments):
            rows = slice(s * PART, (s + 1) * PART)
            re, im = spec[rows, :bins], spec[rows, bins:]
            amp = jnp.sqrt(re * re + im * im)
            top = amp.astype(jnp.bfloat16)
            high[rows, :] = top
            low[rows, :] = (amp - top.astype(jnp.float32)).astype(jnp.bfloat16)
            mean = jnp.sum(amp, axis=1, keepdims=True) * (1.0 / bins)
            water[rows, :] = jnp.broadcast_to(WATER * mean + EPS, (PART, LANES))
        smooth[...] = jnp.dot(high[...], bnd[...], preferred_element_type=jnp.float32) + jnp.dot(
            low[...], bnd[...], preferred_element_type=jnp.float32
        )
        for s in range(segments):
            rows = slice(s * PART, (s + 1) * PART)
            level = water[rows, :]
            for g in range(groups):
                lanes = slice(g * LANES, (g + 1) * LANES)
                scale = 1.0 / jnp.maximum(smooth[rows, lanes] * weight[0:1, lanes], level)
                re = spec[rows, lanes] * scale
                im = spec[rows, slice(bins + g * LANES, bins + (g + 1) * LANES)] * scale
                for h in range(2):
                    share = slice(h * SHARE, (h + 1) * SHARE)
                    both = jnp.concatenate([re[share], im[share]], axis=0)
                    white[i, 2 * g + h, s] = both.astype(jnp.bfloat16)

    def send_row(i):
        for k, mate in enumerate(mates):
            other = lax.rem(place + k + 1, ROW)
            pltpu.make_async_remote_copy(
                white.at[i, other], got.at[i, HALO + place], xs.at[i], xr.at[i], device_id=mate, device_id_type=MESH
            ).start()
        got[i, HALO + place] = white[i, place]

    def row_wait(i):
        block = got.at[i, pl.ds(0, ROW - 1)]
        return pltpu.make_async_remote_copy(block, block, xs.at[i], xr.at[i], device_id=mates[0], device_id_type=MESH)

    def near_copy(i, source, target, device):
        return pltpu.make_async_remote_copy(
            got.at[i, pl.ds(source, HALO)],
            got.at[i, pl.ds(target, HALO)],
            ys.at[i],
            yr.at[i],
            device_id=(device, win),
            device_id_type=MESH,
        )

    def near_wait(i):
        block = got.at[i, pl.ds(0, 2 * HALO)]
        return pltpu.make_async_remote_copy(
            block, block, ys.at[i], yr.at[i], device_id=(above, win), device_id_type=MESH
        )

    def chain_copy(i):
        forth = look_up(i, [int(where > 0) for where, _ in ORDER])
        target = jnp.where(forth == 1, after, before)
        return pltpu.make_async_remote_copy(
            zout.at[i], zin.at[i], zs.at[i], zr.at[i], device_id=(chan, target), device_id_type=MESH
        )

    def cross(i):
        def move(b, carry):
            near[b] = got[i, b]
            return carry

        lax.fori_loop(0, ROW + 2 * HALO, move, 0, unroll=True)

        def owner(j, carry):
            source = [near[HALO + j, s].astype(jnp.float32) for s in range(segments)]
            for p in range(SLOTS):
                receiver = HALO + j + offsets[p, first + j]
                live = p < counts[first + j]
                total_re = jnp.zeros((SHARE, LANES), jnp.float32)
                total_im = jnp.zeros((SHARE, LANES), jnp.float32)
                for s, both in enumerate(source):
                    ar, ai = both[:SHARE], both[SHARE:]
                    other = near[receiver, s].astype(jnp.float32)
                    br, bi = other[:SHARE], other[SHARE:]
                    total_re += ar * br + ai * bi
                    total_im += ar * bi - ai * br
                total = jnp.concatenate([total_re, total_im], axis=0)
                part[SLOTS * j + p] = jnp.where(live, total, 0.0)
            return carry

        lax.fori_loop(0, ROW, owner, 0, unroll=2)

    def add_up(i):
        slot = look_up(i, [max(arrival(step), 0) for step in range(STEPS)])
        joins = look_up(i, [int(arrival(step) >= 0) for step in range(STEPS)]) == 1

        @pl.when(jnp.logical_not(joins))
        def _():
            zout[i] = part[...].astype(jnp.bfloat16)
            chain_copy(i).start()

        @pl.when(joins & (i < OUTSIDE))
        def _():
            chain_copy(slot).wait_recv()
            zout[i] = (part[...] + zin[slot].astype(jnp.float32)).astype(jnp.bfloat16)
            chain_copy(i).start()

        @pl.when(i >= OUTSIDE)
        def _():
            half = i - OUTSIDE
            chain_copy(slot).wait_recv()
            chain_copy(slot + 1).wait_recv()
            total = part[...] + zin[slot].astype(jnp.float32) + zin[slot + 1].astype(jnp.float32)
            fout[half] = total.astype(jnp.bfloat16)
            for k, mate in enumerate(mates):
                other = lax.rem(place + k + 1, ROW)
                pltpu.make_async_remote_copy(
                    fout.at[half, pl.ds(SLOTS * other, SLOTS)],
                    fin.at[half, place],
                    fs.at[half],
                    fr.at[half],
                    device_id=mate,
                    device_id_type=MESH,
                ).start()
            fin[half, place] = fout[half, pl.ds(SLOTS * place, SLOTS)]

    def final_wait(half):
        block = fin.at[half, pl.ds(0, ROW - 1)]
        return pltpu.make_async_remote_copy(
            block, block, fs.at[half], fr.at[half], device_id=mates[0], device_id_type=MESH
        )

    def step(i, carry):
        @pl.when(i < STEPS)
        def _():
            whiten(i)

            @pl.when(i == 0)
            def _():
                pl.semaphore_wait(barrier, len(partners))

            send_row(i)

        @pl.when(i == BEHIND)
        def _():
            tables[3].wait()
            tables[4].wait()

        @pl.when(i >= BEHIND)
        def _():
            near_wait(i - BEHIND).wait_recv()
            cross(i - BEHIND)
            add_up(i - BEHIND)

        @pl.when((i >= AHEAD) & (i < STEPS + AHEAD))
        def _():
            row_wait(i - AHEAD).wait_recv()
            near_copy(i - AHEAD, HALO, HALO + ROW, below).start()
            near_copy(i - AHEAD, ROW, 0, above).start()

        return carry

    lax.fori_loop(0, STEPS + BEHIND, step, 0)

    tables[2].wait()
    for half in range(2):
        final_wait(half).wait_recv()
        for g in range(groups):
            for p in range(SLOTS):
                pieces = [fin[half, 2 * g + h, p].astype(jnp.float32) for h in range(2)]
                re = jnp.concatenate([piece[:SHARE] for piece in pieces], axis=0)
                im = jnp.concatenate([piece[SHARE:] for piece in pieces], axis=0)
                rows = slice(p * PART, (p + 1) * PART)
                left[rows, g * LANES : (g + 1) * LANES] = re.astype(jnp.bfloat16)
                left[rows, bins + g * LANES : bins + (g + 1) * LANES] = im.astype(jnp.bfloat16)
        result = jnp.dot(left[...], inv[...], preferred_element_type=jnp.float32) * norm
        for p in range(SLOTS):
            out[p, half * PART : (half + 1) * PART, :] = result[p * PART : (p + 1) * PART]

    for half in range(2):
        final_wait(half).wait_send()

    def drain(i, carry):
        row_wait(i).wait_send()
        near_wait(i).wait_send()

        @pl.when(i < OUTSIDE)
        def _():
            chain_copy(i).wait_send()

        return carry

    lax.fori_loop(0, STEPS, drain, 0)


def body(traces, offsets, counts):
    segments, channels, length = traces.shape
    bins = length // 2
    norm = 1.0 / math.sqrt(bins * segments * WIN)
    rows = segments * PART
    bf16, f32 = jnp.bfloat16, jnp.float32
    pairs = SLOTS * ROW
    tile = (2 * SHARE, LANES)
    block = (segments,) + tile
    any_space, vmem = pl.BlockSpec(memory_space=pl.ANY), pl.BlockSpec(memory_space=pltpu.VMEM)
    dma = pltpu.SemaphoreType.DMA
    return pl.pallas_call(
        functools.partial(kernel, norm),
        out_shape=jax.ShapeDtypeStruct((SLOTS, channels // WIN, length), f32),
        in_specs=[any_space] * 6,
        out_specs=vmem,
        scratch_shapes=[
            pltpu.SMEM(offsets.shape[::-1], jnp.int32),
            pltpu.SMEM(counts.shape, jnp.int32),
            pltpu.VMEM((STEPS, segments, PART, length), bf16),
            pltpu.VMEM((length, length), bf16),
            pltpu.VMEM((bins, bins), bf16),
            pltpu.VMEM((length, length), bf16),
            pltpu.VMEM((8, bins), f32),
            pltpu.VMEM((rows, length), f32),
            pltpu.VMEM((rows, bins), bf16),
            pltpu.VMEM((rows, bins), bf16),
            pltpu.VMEM((rows, bins), f32),
            pltpu.VMEM((rows, LANES), f32),
            pltpu.VMEM((STEPS, ROW) + block, bf16),
            pltpu.VMEM((STEPS, ROW + 2 * HALO) + block, bf16),
            pltpu.VMEM((ROW + 2 * HALO,) + block, bf16),
            pltpu.VMEM((pairs,) + tile, f32),
            pltpu.VMEM((OUTSIDE, pairs) + tile, bf16),
            pltpu.VMEM((OUTSIDE, pairs) + tile, bf16),
            pltpu.VMEM((2, pairs) + tile, bf16),
            pltpu.VMEM((2, ROW, SLOTS) + tile, bf16),
            pltpu.VMEM((SLOTS * PART, length), bf16),
            dma((5,)),
            dma((STEPS,)),
            dma((STEPS,)),
            dma((STEPS,)),
            dma((STEPS,)),
            dma((STEPS,)),
            dma((OUTSIDE,)),
            dma((OUTSIDE,)),
            dma((2,)),
            dma((2,)),
        ],
        compiler_params=pltpu.CompilerParams(collective_id=0, has_side_effects=True, vmem_limit_bytes=VMEM_BYTES),
    )(
        offsets.T,
        counts,
        traces,
        jnp.asarray(forward_table(length)),
        jnp.asarray(band_table(bins)),
        jnp.asarray(inverse_table(length)),
    )


def solution(mesh):
    in_specs = (P("win", "chan", None), P(), P())
    out_specs = P("chan", "win", None)
    return jax.shard_map(body, mesh=mesh, in_specs=in_specs, out_specs=out_specs, check_vma=False)
```

```python
import functools
import math

import jax
import jax.numpy as jnp
import numpy as np
from jax import lax
from jax.experimental import pallas as pl
from jax.experimental.pallas import tpu as pltpu
from jax.sharding import PartitionSpec as P

MESH = pl.DeviceIdType.MESH
RADIUS = 8
HALO = 3
SLOTS = 3
WATER = 0.8
EPS = 1e-06
ROW = 8
WIN = 8
PART = 16
SHARE = 8
LANES = 128
VMEM_BYTES = 62 << 20

ORDER = [(-4, 0), (-4, 1), (-3, 0), (-3, 1), (3, 0), (3, 1), (-2, 0), (-2, 1), (2, 0), (2, 1)]
ORDER += [(-1, 0), (1, 0), (-1, 1), (1, 1), (0, 0), (0, 1)]
STEPS = len(ORDER)
OUTSIDE = STEPS - 2
WINDOW = 3
LAG = 2


def forward_table(length):
    column = np.arange(length)
    phase = np.arange(length)[:, None] * (column % (length // 2))[None, :] % length
    angles = phase * (2.0 * math.pi / length)
    table = np.where(column[None, :] < length // 2, np.cos(angles), -np.sin(angles))
    return table.astype(jnp.bfloat16)


def inverse_table(length):
    column = np.arange(length)
    phase = np.arange(length)[None, :] * (column % (length // 2))[:, None] % length
    angles = phase * (2.0 * math.pi / length)
    table = np.where(column[:, None] < length // 2, np.cos(angles), -np.sin(angles))
    return table.astype(jnp.bfloat16)


def band_table(bins):
    place = np.arange(bins)
    return (np.abs(place[:, None] - place[None, :]) <= RADIUS).astype(jnp.bfloat16)


def arrival(step):
    where, half = ORDER[step]
    if where in (-4, 3):
        return -1
    return ORDER.index((where - 1 if where <= 0 else where + 1, half))


def toward_first(step, win):
    lower, upper = list(range(STEPS)), list(range(STEPS))
    lower[OUTSIDE - 4 : OUTSIDE] = [ORDER.index(entry) for entry in [(-1, 0), (-1, 1), (1, 0), (1, 1)]]
    upper[OUTSIDE - 4 : OUTSIDE] = [ORDER.index(entry) for entry in [(1, 0), (1, 1), (-1, 0), (-1, 1)]]
    place = jnp.where((win > 0) & (win < WIN // 2), look_up(step, lower), step)
    return jnp.where(win > WIN // 2, look_up(step, upper), place)


def look_up(step, values):
    found = jnp.int32(values[0])
    for k, value in enumerate(values[1:], 1):
        if value != values[0]:
            found = jnp.where(step == k, jnp.int32(value), found)
    return found


def kernel(
    norm, offsets_in, counts_in, traces, forward, band, inverse, out,
    offsets, counts, tr, fwd, bnd, inv, weight, spec, high, low, smooth, water, white, got, near, part, zout, zin,
    fout, fin, left, tab_sem, tr_sem, xs, xr, ys, yr, zs, zr, fs, fr,
):
    segments, bins = tr.shape[1], bnd.shape[0]
    groups = bins // LANES
    chan, win = lax.axis_index("chan"), lax.axis_index("win")
    row, place = chan // ROW, chan % ROW
    first = row * ROW
    above = lax.rem(row + 1, 4) * ROW + place
    below = lax.rem(row + 3, 4) * ROW + place
    after, before = lax.rem(win + 1, WIN), lax.rem(win + WIN - 1, WIN)

    barrier = pltpu.get_barrier_semaphore()
    mates = [(first + lax.rem(place + k, ROW), win) for k in range(1, ROW)]
    partners = mates + [(above, win), (below, win)]
    beside = [(chan, after), (chan, before)]
    odd = win % 2 == 1
    for partner in partners:
        pl.semaphore_signal(barrier, inc=1, device_id=partner, device_id_type=MESH)

    def trace_copy(i):
        entry = toward_first(i, win)
        target = lax.rem(win + look_up(entry, [(where + WIN) % WIN for where, _ in ORDER]), WIN)
        half = look_up(entry, [half for _, half in ORDER])
        rows = pl.ds(pl.multiple_of((2 * target + half) * PART, PART), PART)
        return pltpu.make_async_copy(traces.at[:, rows, :], tr.at[i], tr_sem.at[i])

    tables = [
        pltpu.make_async_copy(source, target, tab_sem.at[k])
        for k, (source, target) in enumerate(
            [(forward, fwd), (band, bnd), (inverse, inv), (offsets_in, offsets), (counts_in, counts)]
        )
    ]
    tables[0].start()
    trace_copy(0).start()
    tables[1].start()

    def start_traces(i, carry):
        trace_copy(i).start()
        return carry

    lax.fori_loop(1, STEPS, start_traces, 0)
    for table in tables[2:]:
        table.start()
    bin_of = lax.broadcasted_iota(jnp.int32, weight.shape, 1)
    count = jnp.minimum(bin_of + RADIUS, bins - 1) - jnp.maximum(bin_of - RADIUS, 0) + 1
    weight[...] = 1.0 / count.astype(jnp.float32)
    tables[0].wait()
    tables[1].wait()

    def whiten(i):
        trace_copy(i).wait()
        lhs = tr[i].reshape(segments * PART, 2 * bins)
        spec[...] = jnp.dot(lhs, fwd[...], preferred_element_type=jnp.float32)
        for s in range(segments):
            rows = slice(s * PART, (s + 1) * PART)
            re, im = spec[rows, :bins], spec[rows, bins:]
            amp = jnp.sqrt(re * re + im * im)
            top = amp.astype(jnp.bfloat16)
            high[rows, :] = top
            low[rows, :] = (amp - top.astype(jnp.float32)).astype(jnp.bfloat16)
            mean = jnp.sum(amp, axis=1, keepdims=True) * (1.0 / bins)
            water[rows, :] = jnp.broadcast_to(WATER * mean + EPS, (PART, LANES))
        smooth[...] = jnp.dot(high[...], bnd[...], preferred_element_type=jnp.float32) + jnp.dot(
            low[...], bnd[...], preferred_element_type=jnp.float32
        )
        for s in range(segments):
            rows = slice(s * PART, (s + 1) * PART)
            level = water[rows, :]
            for g in range(groups):
                lanes = slice(g * LANES, (g + 1) * LANES)
                scale = 1.0 / jnp.maximum(smooth[rows, lanes] * weight[0:1, lanes], level)
                re = spec[rows, lanes] * scale
                im = spec[rows, slice(bins + g * LANES, bins + (g + 1) * LANES)] * scale
                for h in range(2):
                    share = slice(h * SHARE, (h + 1) * SHARE)
                    both = jnp.concatenate([re[share], im[share]], axis=0)
                    white[i, 2 * g + h, s] = both.astype(jnp.bfloat16)

    def send_row(i):
        for k, mate in enumerate(mates):
            other = lax.rem(place + k + 1, ROW)
            pltpu.make_async_remote_copy(
                white.at[i, other], got.at[i, HALO + place], xs.at[i], xr.at[i], device_id=mate, device_id_type=MESH
            ).start()
        got[i, HALO + place] = white[i, place]

    def row_wait(i):
        block = got.at[i, pl.ds(0, ROW - 1)]
        return pltpu.make_async_remote_copy(block, block, xs.at[i], xr.at[i], device_id=mates[0], device_id_type=MESH)

    def near_copy(i, source, target, device):
        return pltpu.make_async_remote_copy(
            got.at[i, pl.ds(source, HALO)],
            got.at[i, pl.ds(target, HALO)],
            ys.at[i],
            yr.at[i],
            device_id=(device, win),
            device_id_type=MESH,
        )

    def near_wait(i):
        block = got.at[i, pl.ds(0, 2 * HALO)]
        return pltpu.make_async_remote_copy(
            block, block, ys.at[i], yr.at[i], device_id=(above, win), device_id_type=MESH
        )

    def chain_copy(i):
        forth = look_up(i, [int(where > 0) for where, _ in ORDER])
        target = jnp.where(forth == 1, after, before)
        return pltpu.make_async_remote_copy(
            zout.at[i], zin.at[i], zs.at[i], zr.at[i], device_id=(chan, target), device_id_type=MESH
        )

    def cross(i):
        def move(b, carry):
            near[b] = got[i, b]
            return carry

        lax.fori_loop(0, ROW + 2 * HALO, move, 0, unroll=True)

        def owner(j, carry):
            source = [near[HALO + j, s].astype(jnp.float32) for s in range(segments)]
            for p in range(SLOTS):
                receiver = HALO + j + offsets[p, first + j]
                live = p < counts[first + j]
                total_re = jnp.zeros((SHARE, LANES), jnp.float32)
                total_im = jnp.zeros((SHARE, LANES), jnp.float32)
                for s, both in enumerate(source):
                    ar, ai = both[:SHARE], both[SHARE:]
                    other = near[receiver, s].astype(jnp.float32)
                    br, bi = other[:SHARE], other[SHARE:]
                    total_re += ar * br + ai * bi
                    total_im += ar * bi - ai * br
                total = jnp.concatenate([total_re, total_im], axis=0)
                part[SLOTS * j + p] = jnp.where(live, total, 0.0)
            return carry

        lax.fori_loop(0, ROW, owner, 0, unroll=2)

    def add_up(i):
        slot = look_up(i, [max(arrival(step), 0) for step in range(STEPS)])
        joins = look_up(i, [int(arrival(step) >= 0) for step in range(STEPS)]) == 1

        @pl.when(jnp.logical_not(joins))
        def _():
            zout[i] = part[...].astype(jnp.bfloat16)
            chain_copy(i).start()

        @pl.when(joins & (i < OUTSIDE))
        def _():
            chain_copy(slot).wait_recv()
            zout[i] = (part[...] + zin[slot].astype(jnp.float32)).astype(jnp.bfloat16)
            chain_copy(i).start()

        @pl.when(i >= OUTSIDE)
        def _():
            half = i - OUTSIDE
            chain_copy(slot).wait_recv()
            chain_copy(slot + 1).wait_recv()
            total = part[...] + zin[slot].astype(jnp.float32) + zin[slot + 1].astype(jnp.float32)
            fout[half] = total.astype(jnp.bfloat16)
            for k, mate in enumerate(mates):
                other = lax.rem(place + k + 1, ROW)
                pltpu.make_async_remote_copy(
                    fout.at[half, pl.ds(SLOTS * other, SLOTS)],
                    fin.at[half, place],
                    fs.at[half],
                    fr.at[half],
                    device_id=mate,
                    device_id_type=MESH,
                ).start()
            fin[half, place] = fout[half, pl.ds(SLOTS * place, SLOTS)]

    def final_wait(half):
        block = fin.at[half, pl.ds(0, ROW - 1)]
        return pltpu.make_async_remote_copy(
            block, block, fs.at[half], fr.at[half], device_id=mates[0], device_id_type=MESH
        )

    def step(n, carry):
        send, arrived, paired = n - 1, n - 1 - WINDOW, n - 1 - WINDOW - LAG

        @pl.when((arrived >= 0) & (arrived < STEPS))
        def _():
            row_wait(arrived).wait_recv()

        @pl.when(send == 0)
        def _():
            pl.semaphore_wait(barrier, len(partners) + jnp.where(odd, len(beside), 0))
            for partner in beside:
                pl.semaphore_signal(barrier, inc=1, device_id=partner, device_id_type=MESH)

        @pl.when((send >= 0) & (send < STEPS))
        def _():
            send_row(send)

        @pl.when((arrived >= 0) & (arrived < STEPS))
        def _():
            near_copy(arrived, HALO, HALO + ROW, below).start()
            near_copy(arrived, ROW, 0, above).start()

        @pl.when(n < STEPS)
        def _():
            whiten(n)

        @pl.when(paired == 0)
        def _():
            tables[3].wait()
            tables[4].wait()

            @pl.when(jnp.logical_not(odd))
            def _():
                pl.semaphore_wait(barrier, len(beside))

        @pl.when(paired >= 0)
        def _():
            near_wait(paired).wait_recv()
            cross(paired)
            add_up(toward_first(paired, win))

        return carry

    lax.fori_loop(0, STEPS + 1 + WINDOW + LAG, step, 0)

    tables[2].wait()
    for half in range(2):
        final_wait(half).wait_recv()
        for g in range(groups):
            for p in range(SLOTS):
                pieces = [fin[half, 2 * g + h, p].astype(jnp.float32) for h in range(2)]
                re = jnp.concatenate([piece[:SHARE] for piece in pieces], axis=0)
                im = jnp.concatenate([piece[SHARE:] for piece in pieces], axis=0)
                rows = slice(p * PART, (p + 1) * PART)
                left[rows, g * LANES : (g + 1) * LANES] = re.astype(jnp.bfloat16)
                left[rows, bins + g * LANES : bins + (g + 1) * LANES] = im.astype(jnp.bfloat16)
        result = jnp.dot(left[...], inv[...], preferred_element_type=jnp.float32) * norm
        for p in range(SLOTS):
            out[p, half * PART : (half + 1) * PART, :] = result[p * PART : (p + 1) * PART]

    for half in range(2):
        final_wait(half).wait_send()

    def drain(i, carry):
        row_wait(i).wait_send()
        near_wait(i).wait_send()

        @pl.when(i < OUTSIDE)
        def _():
            chain_copy(i).wait_send()

        return carry

    lax.fori_loop(0, STEPS, drain, 0)


def body(traces, offsets, counts):
    segments, channels, length = traces.shape
    bins = length // 2
    norm = 1.0 / math.sqrt(bins * segments * WIN)
    rows = segments * PART
    bf16, f32 = jnp.bfloat16, jnp.float32
    pairs = SLOTS * ROW
    tile = (2 * SHARE, LANES)
    block = (segments,) + tile
    any_space, vmem = pl.BlockSpec(memory_space=pl.ANY), pl.BlockSpec(memory_space=pltpu.VMEM)
    dma = pltpu.SemaphoreType.DMA
    return pl.pallas_call(
        functools.partial(kernel, norm),
        out_shape=jax.ShapeDtypeStruct((SLOTS, channels // WIN, length), f32),
        in_specs=[any_space] * 6,
        out_specs=vmem,
        scratch_shapes=[
            pltpu.SMEM(offsets.shape[::-1], jnp.int32),
            pltpu.SMEM(counts.shape, jnp.int32),
            pltpu.VMEM((STEPS, segments, PART, length), bf16),
            pltpu.VMEM((length, length), bf16),
            pltpu.VMEM((bins, bins), bf16),
            pltpu.VMEM((length, length), bf16),
            pltpu.VMEM((8, bins), f32),
            pltpu.VMEM((rows, length), f32),
            pltpu.VMEM((rows, bins), bf16),
            pltpu.VMEM((rows, bins), bf16),
            pltpu.VMEM((rows, bins), f32),
            pltpu.VMEM((rows, LANES), f32),
            pltpu.VMEM((STEPS, ROW) + block, bf16),
            pltpu.VMEM((STEPS, ROW + 2 * HALO) + block, bf16),
            pltpu.VMEM((ROW + 2 * HALO,) + block, bf16),
            pltpu.VMEM((pairs,) + tile, f32),
            pltpu.VMEM((OUTSIDE, pairs) + tile, bf16),
            pltpu.VMEM((OUTSIDE, pairs) + tile, bf16),
            pltpu.VMEM((2, pairs) + tile, bf16),
            pltpu.VMEM((2, ROW, SLOTS) + tile, bf16),
            pltpu.VMEM((SLOTS * PART, length), bf16),
            dma((5,)),
            dma((STEPS,)),
            dma((STEPS,)),
            dma((STEPS,)),
            dma((STEPS,)),
            dma((STEPS,)),
            dma((OUTSIDE,)),
            dma((OUTSIDE,)),
            dma((2,)),
            dma((2,)),
        ],
        compiler_params=pltpu.CompilerParams(collective_id=0, has_side_effects=True, vmem_limit_bytes=VMEM_BYTES),
    )(
        offsets.T,
        counts,
        traces,
        jnp.asarray(forward_table(length)),
        jnp.asarray(band_table(bins)),
        jnp.asarray(inverse_table(length)),
    )


def solution(mesh):
    in_specs = (P("win", "chan", None), P(), P())
    out_specs = P("chan", "win", None)
    return jax.shard_map(body, mesh=mesh, in_specs=in_specs, out_specs=out_specs, check_vma=False)
```

```python
import functools
import math

import jax
import jax.numpy as jnp
import numpy as np
from jax import lax
from jax.experimental import pallas as pl
from jax.experimental.pallas import tpu as pltpu
from jax.sharding import PartitionSpec as P

MESH = pl.DeviceIdType.MESH
RADIUS = 8
HALO = 3
SLOTS = 3
WATER = 0.8
EPS = 1e-06
ROW = 8
WIN = 8
PART = 16
SHARE = 8
LANES = 128
VMEM_BYTES = 62 << 20

ORDER = [(where, half) for where in (-4, 3, -3, 2, -2, 1, -1, 0) for half in (0, 1)]
STEPS = len(ORDER)
OUTSIDE = STEPS - 2
GREETED = [0, 1, 2, 0, 2, 0, 2, 1]
CUTS = 2
WINDOW = 3
LAG = 2


def forward_table(length):
    column = np.arange(length)
    phase = np.arange(length)[:, None] * (column % (length // 2))[None, :] % length
    angles = phase * (2.0 * math.pi / length)
    table = np.where(column[None, :] < length // 2, np.cos(angles), -np.sin(angles))
    return table.astype(jnp.bfloat16)


def inverse_table(length):
    column = np.arange(length)
    phase = np.arange(length)[None, :] * (column % (length // 2))[:, None] % length
    angles = phase * (2.0 * math.pi / length)
    table = np.where(column[:, None] < length // 2, np.cos(angles), -np.sin(angles))
    return table.astype(jnp.bfloat16)


def band_table(bins):
    place = np.arange(bins)
    return (np.abs(place[:, None] - place[None, :]) <= RADIUS).astype(jnp.bfloat16)


def arrival(step):
    where, half = ORDER[step]
    if where in (-4, 3):
        return -1
    return ORDER.index((where - 1 if where <= 0 else where + 1, half))


def entry_of(step, win):
    nearest = list(range(OUTSIDE - 4)) + [OUTSIDE - 2, OUTSIDE - 1, OUTSIDE - 4, OUTSIDE - 3, STEPS - 2, STEPS - 1]
    second = list(range(OUTSIDE - 8)) + [OUTSIDE - 6, OUTSIDE - 5, OUTSIDE - 8, OUTSIDE - 7]
    second += nearest[OUTSIDE - 4 :]
    place = jnp.where((win == 1) | (win == 4), look_up(step, nearest), step)
    return jnp.where(win == 2, look_up(step, second), place)


def look_up(step, values):
    found = jnp.int32(values[0])
    for k, value in enumerate(values[1:], 1):
        if value != values[0]:
            found = jnp.where(step == k, jnp.int32(value), found)
    return found


def kernel(
    norm, offsets_in, counts_in, traces, forward, band, inverse, out,
    offsets, counts, tr, fwd, bnd, inv, weight, spec, high, low, smooth, water, white, got, near, part, zout, zin,
    fout, fin, left, tab_sem, tr_sem, xs, xr, ys, yr, zs, zr, fs, fr,
):
    segments, bins = tr.shape[1], bnd.shape[0]
    groups = bins // LANES
    chan, win = lax.axis_index("chan"), lax.axis_index("win")
    row, place = chan // ROW, chan % ROW
    first = row * ROW
    above = lax.rem(row + 1, 4) * ROW + place
    below = lax.rem(row + 3, 4) * ROW + place
    after, before = lax.rem(win + 1, WIN), lax.rem(win + WIN - 1, WIN)

    barrier = pltpu.get_barrier_semaphore()
    mates = [(first + lax.rem(place + k, ROW), win) for k in range(1, ROW)]
    partners = mates + [(above, win), (below, win)]
    beside = [(chan, after), (chan, before)]
    greeted = look_up(win, GREETED)
    for partner in partners:
        pl.semaphore_signal(barrier, inc=1, device_id=partner, device_id_type=MESH)

    def trace_copy(i):
        entry = entry_of(i, win)
        target = lax.rem(win + look_up(entry, [(where + WIN) % WIN for where, _ in ORDER]), WIN)
        half = look_up(entry, [half for _, half in ORDER])
        rows = pl.ds(pl.multiple_of((2 * target + half) * PART, PART), PART)
        return pltpu.make_async_copy(traces.at[:, rows, :], tr.at[i], tr_sem.at[i])

    tables = [
        pltpu.make_async_copy(source, target, tab_sem.at[k])
        for k, (source, target) in enumerate(
            [(forward, fwd), (band, bnd), (inverse, inv), (offsets_in, offsets), (counts_in, counts)]
        )
    ]
    tables[0].start()
    trace_copy(0).start()
    tables[1].start()

    def start_traces(i, carry):
        trace_copy(i).start()
        return carry

    lax.fori_loop(1, STEPS, start_traces, 0)
    for table in tables[2:]:
        table.start()
    bin_of = lax.broadcasted_iota(jnp.int32, weight.shape, 1)
    count = jnp.minimum(bin_of + RADIUS, bins - 1) - jnp.maximum(bin_of - RADIUS, 0) + 1
    weight[...] = 1.0 / count.astype(jnp.float32)
    tables[0].wait()
    tables[1].wait()

    def whiten(i):
        trace_copy(i).wait()
        lhs = tr[i].reshape(segments * PART, 2 * bins)
        spec[...] = jnp.dot(lhs, fwd[...], preferred_element_type=jnp.float32)
        for s in range(segments):
            rows = slice(s * PART, (s + 1) * PART)
            re, im = spec[rows, :bins], spec[rows, bins:]
            amp = jnp.sqrt(re * re + im * im)
            top = amp.astype(jnp.bfloat16)
            high[rows, :] = top
            low[rows, :] = (amp - top.astype(jnp.float32)).astype(jnp.bfloat16)
            mean = jnp.sum(amp, axis=1, keepdims=True) * (1.0 / bins)
            water[rows, :] = jnp.broadcast_to(WATER * mean + EPS, (PART, LANES))
        smooth[...] = jnp.dot(high[...], bnd[...], preferred_element_type=jnp.float32) + jnp.dot(
            low[...], bnd[...], preferred_element_type=jnp.float32
        )
        for s in range(segments):
            rows = slice(s * PART, (s + 1) * PART)
            level = water[rows, :]
            for g in range(groups):
                lanes = slice(g * LANES, (g + 1) * LANES)
                scale = 1.0 / jnp.maximum(smooth[rows, lanes] * weight[0:1, lanes], level)
                re = spec[rows, lanes] * scale
                im = spec[rows, slice(bins + g * LANES, bins + (g + 1) * LANES)] * scale
                for h in range(2):
                    share = slice(h * SHARE, (h + 1) * SHARE)
                    both = jnp.concatenate([re[share], im[share]], axis=0)
                    white[i, s // (segments // CUTS), 2 * g + h, s % (segments // CUTS)] = both.astype(jnp.bfloat16)

    def send_row(i, c):
        for k, mate in enumerate(mates):
            other = lax.rem(place + k + 1, ROW)
            pltpu.make_async_remote_copy(
                white.at[i, c, other],
                got.at[i, c, HALO + place],
                xs.at[i, c],
                xr.at[i, c],
                device_id=mate,
                device_id_type=MESH,
            ).start()

    def row_wait(i, c):
        block = got.at[i, c, pl.ds(0, ROW - 1)]
        return pltpu.make_async_remote_copy(
            block, block, xs.at[i, c], xr.at[i, c], device_id=mates[0], device_id_type=MESH
        )

    def near_copy(i, c, source, target, device):
        return pltpu.make_async_remote_copy(
            got.at[i, c, pl.ds(source, HALO)],
            got.at[i, c, pl.ds(target, HALO)],
            ys.at[i, c],
            yr.at[i, c],
            device_id=(device, win),
            device_id_type=MESH,
        )

    def near_wait(i, c):
        block = got.at[i, c, pl.ds(0, 2 * HALO)]
        return pltpu.make_async_remote_copy(
            block, block, ys.at[i, c], yr.at[i, c], device_id=(above, win), device_id_type=MESH
        )

    def chain_copy(i):
        forth = look_up(i, [int(where > 0) for where, _ in ORDER])
        target = jnp.where(forth == 1, after, before)
        return pltpu.make_async_remote_copy(
            zout.at[i], zin.at[i], zs.at[i], zr.at[i], device_id=(chan, target), device_id_type=MESH
        )

    def cross(i):
        def move(b, carry):
            for c in range(CUTS):
                near[b, pl.ds(c * (segments // CUTS), segments // CUTS)] = got[i, c, b]
            return carry

        lax.fori_loop(0, ROW + 2 * HALO, move, 0, unroll=True)

        def owner(j, carry):
            source = [near[HALO + j, s].astype(jnp.float32) for s in range(segments)]
            for p in range(SLOTS):
                receiver = HALO + j + offsets[p, first + j]
                live = p < counts[first + j]
                total_re = jnp.zeros((SHARE, LANES), jnp.float32)
                total_im = jnp.zeros((SHARE, LANES), jnp.float32)
                for s, both in enumerate(source):
                    ar, ai = both[:SHARE], both[SHARE:]
                    other = near[receiver, s].astype(jnp.float32)
                    br, bi = other[:SHARE], other[SHARE:]
                    total_re += ar * br + ai * bi
                    total_im += ar * bi - ai * br
                total = jnp.concatenate([total_re, total_im], axis=0)
                part[SLOTS * j + p] = jnp.where(live, total, 0.0)
            return carry

        lax.fori_loop(0, ROW, owner, 0, unroll=2)

    def add_up(i):
        slot = look_up(i, [max(arrival(step), 0) for step in range(STEPS)])
        joins = look_up(i, [int(arrival(step) >= 0) for step in range(STEPS)]) == 1

        @pl.when(jnp.logical_not(joins))
        def _():
            zout[i] = part[...].astype(jnp.bfloat16)
            chain_copy(i).start()

        @pl.when(joins & (i < OUTSIDE))
        def _():
            chain_copy(slot).wait_recv()
            zout[i] = (part[...] + zin[slot].astype(jnp.float32)).astype(jnp.bfloat16)
            chain_copy(i).start()

        @pl.when(i >= OUTSIDE)
        def _():
            half = i - OUTSIDE
            chain_copy(slot).wait_recv()
            chain_copy(slot - 2).wait_recv()
            total = part[...] + zin[slot].astype(jnp.float32) + zin[slot - 2].astype(jnp.float32)
            fout[half] = total.astype(jnp.bfloat16)
            for k, mate in enumerate(mates):
                other = lax.rem(place + k + 1, ROW)
                pltpu.make_async_remote_copy(
                    fout.at[half, pl.ds(SLOTS * other, SLOTS)],
                    fin.at[half, place],
                    fs.at[half],
                    fr.at[half],
                    device_id=mate,
                    device_id_type=MESH,
                ).start()
            fin[half, place] = fout[half, pl.ds(SLOTS * place, SLOTS)]

    def final_wait(half):
        block = fin.at[half, pl.ds(0, ROW - 1)]
        return pltpu.make_async_remote_copy(
            block, block, fs.at[half], fr.at[half], device_id=mates[0], device_id_type=MESH
        )

    def step(n, carry):
        send, arrived, paired = n - 1, n - 1 - WINDOW, n - 1 - WINDOW - LAG

        @pl.when(send == 0)
        def _():
            pl.semaphore_wait(barrier, len(partners) + greeted)
            for partner in beside:
                pl.semaphore_signal(barrier, inc=1, device_id=partner, device_id_type=MESH)

        @pl.when((arrived >= 0) & (arrived < STEPS))
        def _():
            for c in range(CUTS):
                row_wait(arrived, c).wait_recv()
                near_copy(arrived, c, HALO, HALO + ROW, below).start()
                near_copy(arrived, c, ROW, 0, above).start()

        @pl.when((send >= 0) & (send < STEPS))
        def _():
            for c in range(CUTS):
                send_row(send, c)
            for c in range(CUTS):
                got[send, c, HALO + place] = white[send, c, place]

        @pl.when(n < STEPS)
        def _():
            whiten(n)

        @pl.when(paired == 0)
        def _():
            tables[3].wait()
            tables[4].wait()

            @pl.when(greeted < len(beside))
            def _():
                pl.semaphore_wait(barrier, len(beside) - greeted)

        @pl.when(paired >= 0)
        def _():
            for c in range(CUTS):
                near_wait(paired, c).wait_recv()
            cross(paired)
            add_up(entry_of(paired, win))

        return carry

    lax.fori_loop(0, STEPS + 1 + WINDOW + LAG, step, 0)

    tables[2].wait()
    for half in range(2):
        final_wait(half).wait_recv()
        for g in range(groups):
            for p in range(SLOTS):
                pieces = [fin[half, 2 * g + h, p].astype(jnp.float32) for h in range(2)]
                re = jnp.concatenate([piece[:SHARE] for piece in pieces], axis=0)
                im = jnp.concatenate([piece[SHARE:] for piece in pieces], axis=0)
                rows = slice(p * PART, (p + 1) * PART)
                left[rows, g * LANES : (g + 1) * LANES] = re.astype(jnp.bfloat16)
                left[rows, bins + g * LANES : bins + (g + 1) * LANES] = im.astype(jnp.bfloat16)
        result = jnp.dot(left[...], inv[...], preferred_element_type=jnp.float32) * norm
        for p in range(SLOTS):
            out[p, half * PART : (half + 1) * PART, :] = result[p * PART : (p + 1) * PART]

    for half in range(2):
        final_wait(half).wait_send()

    def drain(i, carry):
        for c in range(CUTS):
            row_wait(i, c).wait_send()
            near_wait(i, c).wait_send()

        @pl.when(i < OUTSIDE)
        def _():
            chain_copy(i).wait_send()

        return carry

    lax.fori_loop(0, STEPS, drain, 0)


def body(traces, offsets, counts):
    segments, channels, length = traces.shape
    bins = length // 2
    norm = 1.0 / math.sqrt(bins * segments * WIN)
    rows = segments * PART
    bf16, f32 = jnp.bfloat16, jnp.float32
    pairs = SLOTS * ROW
    tile = (2 * SHARE, LANES)
    block = (segments,) + tile
    cut = (segments // CUTS,) + tile
    any_space, vmem = pl.BlockSpec(memory_space=pl.ANY), pl.BlockSpec(memory_space=pltpu.VMEM)
    dma = pltpu.SemaphoreType.DMA
    return pl.pallas_call(
        functools.partial(kernel, norm),
        out_shape=jax.ShapeDtypeStruct((SLOTS, channels // WIN, length), f32),
        in_specs=[any_space] * 6,
        out_specs=vmem,
        scratch_shapes=[
            pltpu.SMEM(offsets.shape[::-1], jnp.int32),
            pltpu.SMEM(counts.shape, jnp.int32),
            pltpu.VMEM((STEPS, segments, PART, length), bf16),
            pltpu.VMEM((length, length), bf16),
            pltpu.VMEM((bins, bins), bf16),
            pltpu.VMEM((length, length), bf16),
            pltpu.VMEM((8, bins), f32),
            pltpu.VMEM((rows, length), f32),
            pltpu.VMEM((rows, bins), bf16),
            pltpu.VMEM((rows, bins), bf16),
            pltpu.VMEM((rows, bins), f32),
            pltpu.VMEM((rows, LANES), f32),
            pltpu.VMEM((STEPS, CUTS, ROW) + cut, bf16),
            pltpu.VMEM((STEPS, CUTS, ROW + 2 * HALO) + cut, bf16),
            pltpu.VMEM((ROW + 2 * HALO,) + block, bf16),
            pltpu.VMEM((pairs,) + tile, f32),
            pltpu.VMEM((OUTSIDE, pairs) + tile, bf16),
            pltpu.VMEM((OUTSIDE, pairs) + tile, bf16),
            pltpu.VMEM((2, pairs) + tile, bf16),
            pltpu.VMEM((2, ROW, SLOTS) + tile, bf16),
            pltpu.VMEM((SLOTS * PART, length), bf16),
            dma((5,)),
            dma((STEPS,)),
            dma((STEPS, CUTS)),
            dma((STEPS, CUTS)),
            dma((STEPS, CUTS)),
            dma((STEPS, CUTS)),
            dma((OUTSIDE,)),
            dma((OUTSIDE,)),
            dma((2,)),
            dma((2,)),
        ],
        compiler_params=pltpu.CompilerParams(collective_id=0, has_side_effects=True, vmem_limit_bytes=VMEM_BYTES),
    )(
        offsets.T,
        counts,
        traces,
        jnp.asarray(forward_table(length)),
        jnp.asarray(band_table(bins)),
        jnp.asarray(inverse_table(length)),
    )


def solution(mesh):
    in_specs = (P("win", "chan", None), P(), P())
    out_specs = P("chan", "win", None)
    return jax.shard_map(body, mesh=mesh, in_specs=in_specs, out_specs=out_specs, check_vma=False)
```

```python
import functools
import math

import jax
import jax.numpy as jnp
import numpy as np
from jax import lax
from jax.experimental import pallas as pl
from jax.experimental.pallas import tpu as pltpu
from jax.sharding import PartitionSpec as P

MESH = pl.DeviceIdType.MESH
RADIUS = 8
HALO = 3
SLOTS = 3
WATER = 0.8
EPS = 1e-06
ROW = 8
WIN = 8
PART = 16
SHARE = 8
LANES = 128
VMEM_BYTES = 107 << 19

ORDER = [(where, half) for where in (-4, 3, -3, 2, -2, 1, -1, 0) for half in (0, 1)]
STEPS = len(ORDER)
OUTSIDE = STEPS - 2
GREETED = [0, 1, 2, 0, 2, 0, 2, 1]
CUTS = 2
WINDOW = 3
LAG = 2


def forward_table(length):
    column = np.arange(length)
    phase = np.arange(length)[:, None] * (column % (length // 2))[None, :] % length
    angles = phase * (2.0 * math.pi / length)
    table = np.where(column[None, :] < length // 2, np.cos(angles), -np.sin(angles))
    return table.astype(jnp.bfloat16)


def inverse_table(length):
    column = np.arange(length)
    phase = np.arange(length)[None, :] * (column % (length // 2))[:, None] % length
    angles = phase * (2.0 * math.pi / length)
    table = np.where(column[:, None] < length // 2, np.cos(angles), -np.sin(angles))
    return table.astype(jnp.bfloat16)


def band_table(bins):
    place = np.arange(bins)
    return (np.abs(place[:, None] - place[None, :]) <= RADIUS).astype(jnp.bfloat16)


def arrival(step):
    where, half = ORDER[step]
    if where in (-4, 3):
        return -1
    return ORDER.index((where - 1 if where <= 0 else where + 1, half))


def entry_of(step, win):
    nearest = list(range(OUTSIDE - 4)) + [OUTSIDE - 2, OUTSIDE - 1, OUTSIDE - 4, OUTSIDE - 3, STEPS - 2, STEPS - 1]
    second = list(range(OUTSIDE - 8)) + [OUTSIDE - 6, OUTSIDE - 5, OUTSIDE - 8, OUTSIDE - 7]
    second += nearest[OUTSIDE - 4 :]
    place = jnp.where((win == 1) | (win == 4), look_up(step, nearest), step)
    return jnp.where(win == 2, look_up(step, second), place)


def look_up(step, values):
    found = jnp.int32(values[0])
    for k, value in enumerate(values[1:], 1):
        if value != values[0]:
            found = jnp.where(step == k, jnp.int32(value), found)
    return found


def kernel(
    norm, pairs_in, traces, forward, band, inverse, out,
    pairs, tr, fwd, bnd, inv, weight, spec, high, low, smooth, water, white, got, near, part, zout, zin,
    fout, fin, left, tab_sem, tr_sem, xs, xr, ys, yr, zs, zr, fs, fr,
):
    segments, bins = tr.shape[1], bnd.shape[0]
    groups = bins // LANES
    chan, win = lax.axis_index("chan"), lax.axis_index("win")
    row, place = chan // ROW, chan % ROW
    first = row * ROW
    above = lax.rem(row + 1, 4) * ROW + place
    below = lax.rem(row + 3, 4) * ROW + place
    after, before = lax.rem(win + 1, WIN), lax.rem(win + WIN - 1, WIN)

    barrier = pltpu.get_barrier_semaphore()
    mates = [(first + lax.rem(place + k, ROW), win) for k in range(1, ROW)]
    partners = mates + [(above, win), (below, win)]
    beside = [(chan, after), (chan, before)]
    greeted = look_up(win, GREETED)
    for partner in partners:
        pl.semaphore_signal(barrier, inc=1, device_id=partner, device_id_type=MESH)

    def trace_copy(i):
        entry = entry_of(i, win)
        target = lax.rem(win + look_up(entry, [(where + WIN) % WIN for where, _ in ORDER]), WIN)
        half = look_up(entry, [half for _, half in ORDER])
        rows = pl.ds(pl.multiple_of((2 * target + half) * PART, PART), PART)
        return pltpu.make_async_copy(traces.at[:, rows, :], tr.at[i], tr_sem.at[i])

    tables = [
        pltpu.make_async_copy(source, target, tab_sem.at[k])
        for k, (source, target) in enumerate(
            [(forward, fwd), (band, bnd), (inverse, inv), (pairs_in, pairs)]
        )
    ]
    tables[0].start()
    trace_copy(0).start()
    tables[1].start()

    def start_traces(i, carry):
        trace_copy(i).start()
        return carry

    lax.fori_loop(1, STEPS, start_traces, 0)
    for table in tables[2:]:
        table.start()
    bin_of = lax.broadcasted_iota(jnp.int32, weight.shape, 1)
    count = jnp.minimum(bin_of + RADIUS, bins - 1) - jnp.maximum(bin_of - RADIUS, 0) + 1
    weight[...] = 1.0 / count.astype(jnp.float32)
    tables[0].wait()
    tables[1].wait()

    def whiten(i):
        trace_copy(i).wait()
        lhs = tr[i].reshape(segments * PART, 2 * bins)
        spec[...] = jnp.dot(lhs, fwd[...], preferred_element_type=jnp.float32)
        for s in range(segments):
            rows = slice(s * PART, (s + 1) * PART)
            re, im = spec[rows, :bins], spec[rows, bins:]
            amp = jnp.sqrt(re * re + im * im)
            top = amp.astype(jnp.bfloat16)
            high[rows, :] = top
            low[rows, :] = (amp - top.astype(jnp.float32)).astype(jnp.bfloat16)
            mean = jnp.sum(amp, axis=1, keepdims=True) * (1.0 / bins)
            water[rows, :] = jnp.broadcast_to(WATER * mean + EPS, (PART, LANES))
        smooth[...] = jnp.dot(high[...], bnd[...], preferred_element_type=jnp.float32) + jnp.dot(
            low[...], bnd[...], preferred_element_type=jnp.float32
        )
        for s in range(segments):
            rows = slice(s * PART, (s + 1) * PART)
            level = water[rows, :]
            for g in range(groups):
                lanes = slice(g * LANES, (g + 1) * LANES)
                scale = 1.0 / jnp.maximum(smooth[rows, lanes] * weight[0:1, lanes], level)
                re = spec[rows, lanes] * scale
                im = spec[rows, slice(bins + g * LANES, bins + (g + 1) * LANES)] * scale
                for h in range(2):
                    share = slice(h * SHARE, (h + 1) * SHARE)
                    both = jnp.concatenate([re[share], im[share]], axis=0)
                    white[i, s // (segments // CUTS), 2 * g + h, s % (segments // CUTS)] = both.astype(jnp.bfloat16)

    def send_row(i, c):
        for k, mate in enumerate(mates):
            other = lax.rem(place + k + 1, ROW)
            pltpu.make_async_remote_copy(
                white.at[i, c, other],
                got.at[i, c, HALO + place],
                xs.at[i, c],
                xr.at[i, c],
                device_id=mate,
                device_id_type=MESH,
            ).start()

    def row_wait(i, c):
        block = got.at[i, c, pl.ds(0, ROW - 1)]
        return pltpu.make_async_remote_copy(
            block, block, xs.at[i, c], xr.at[i, c], device_id=mates[0], device_id_type=MESH
        )

    def near_copy(i, c, source, target, device):
        return pltpu.make_async_remote_copy(
            got.at[i, c, pl.ds(source, HALO)],
            got.at[i, c, pl.ds(target, HALO)],
            ys.at[i, c],
            yr.at[i, c],
            device_id=(device, win),
            device_id_type=MESH,
        )

    def near_wait(i, c):
        block = got.at[i, c, pl.ds(0, 2 * HALO)]
        return pltpu.make_async_remote_copy(
            block, block, ys.at[i, c], yr.at[i, c], device_id=(above, win), device_id_type=MESH
        )

    def chain_copy(i):
        forth = look_up(i, [int(where > 0) for where, _ in ORDER])
        target = jnp.where(forth == 1, after, before)
        return pltpu.make_async_remote_copy(
            zout.at[i], zin.at[i], zs.at[i], zr.at[i], device_id=(chan, target), device_id_type=MESH
        )

    def cross(i):
        def move(b, carry):
            for c in range(CUTS):
                near[b, pl.ds(c * (segments // CUTS), segments // CUTS)] = got[i, c, b]
            return carry

        lax.fori_loop(0, ROW + 2 * HALO, move, 0, unroll=True)

        def owner(j, carry):
            source = [near[HALO + j, s].astype(jnp.float32) for s in range(segments)]
            for p in range(SLOTS):
                receiver = HALO + j + pairs[p, first + j]
                live = p < pairs[SLOTS, first + j]
                total_re = jnp.zeros((SHARE, LANES), jnp.float32)
                total_im = jnp.zeros((SHARE, LANES), jnp.float32)
                for s, both in enumerate(source):
                    ar, ai = both[:SHARE], both[SHARE:]
                    other = near[receiver, s].astype(jnp.float32)
                    br, bi = other[:SHARE], other[SHARE:]
                    total_re += ar * br + ai * bi
                    total_im += ar * bi - ai * br
                total = jnp.concatenate([total_re, total_im], axis=0)
                part[SLOTS * j + p] = jnp.where(live, total, 0.0)
            return carry

        lax.fori_loop(0, ROW, owner, 0, unroll=2)

    def add_up(i):
        slot = look_up(i, [max(arrival(step), 0) for step in range(STEPS)])
        joins = look_up(i, [int(arrival(step) >= 0) for step in range(STEPS)]) == 1

        @pl.when(jnp.logical_not(joins))
        def _():
            zout[i] = part[...].astype(jnp.bfloat16)
            chain_copy(i).start()

        @pl.when(joins & (i < OUTSIDE))
        def _():
            chain_copy(slot).wait_recv()
            zout[i] = (part[...] + zin[slot].astype(jnp.float32)).astype(jnp.bfloat16)
            chain_copy(i).start()

        @pl.when(i >= OUTSIDE)
        def _():
            half = i - OUTSIDE
            chain_copy(slot).wait_recv()
            chain_copy(slot - 2).wait_recv()
            total = part[...] + zin[slot].astype(jnp.float32) + zin[slot - 2].astype(jnp.float32)
            fout[half] = total.astype(jnp.bfloat16)
            for k, mate in enumerate(mates):
                other = lax.rem(place + k + 1, ROW)
                pltpu.make_async_remote_copy(
                    fout.at[half, pl.ds(SLOTS * other, SLOTS)],
                    fin.at[half, place],
                    fs.at[half],
                    fr.at[half],
                    device_id=mate,
                    device_id_type=MESH,
                ).start()
            fin[half, place] = fout[half, pl.ds(SLOTS * place, SLOTS)]

    def final_wait(half):
        block = fin.at[half, pl.ds(0, ROW - 1)]
        return pltpu.make_async_remote_copy(
            block, block, fs.at[half], fr.at[half], device_id=mates[0], device_id_type=MESH
        )

    def step(n, carry):
        send, arrived, paired = n - 1, n - 1 - WINDOW, n - 1 - WINDOW - LAG

        @pl.when(send == 0)
        def _():
            pl.semaphore_wait(barrier, len(partners) + greeted)
            for partner in beside:
                pl.semaphore_signal(barrier, inc=1, device_id=partner, device_id_type=MESH)

        @pl.when((arrived >= 0) & (arrived < STEPS))
        def _():
            for c in range(CUTS):
                row_wait(arrived, c).wait_recv()
                near_copy(arrived, c, HALO, HALO + ROW, below).start()
                near_copy(arrived, c, ROW, 0, above).start()

        @pl.when((send >= 0) & (send < STEPS))
        def _():
            for c in range(CUTS):
                send_row(send, c)
            for c in range(CUTS):
                got[send, c, HALO + place] = white[send, c, place]

        @pl.when(n < STEPS)
        def _():
            whiten(n)

        @pl.when(paired == 0)
        def _():
            tables[3].wait()

            @pl.when(greeted < len(beside))
            def _():
                pl.semaphore_wait(barrier, len(beside) - greeted)

        @pl.when(paired >= 0)
        def _():
            for c in range(CUTS):
                near_wait(paired, c).wait_recv()
            cross(paired)
            add_up(entry_of(paired, win))

        return carry

    lax.fori_loop(0, STEPS + 1 + WINDOW + LAG, step, 0)

    def drain(i, carry):
        for c in range(CUTS):
            row_wait(i, c).wait_send()
            near_wait(i, c).wait_send()

        @pl.when(i < OUTSIDE)
        def _():
            chain_copy(i).wait_send()

        return carry

    lax.fori_loop(0, STEPS, drain, 0)

    tables[2].wait()
    for half in range(2):
        final_wait(half).wait_recv()
        for g in range(groups):
            for p in range(SLOTS):
                pieces = [fin[half, 2 * g + h, p].astype(jnp.float32) for h in range(2)]
                re = jnp.concatenate([piece[:SHARE] for piece in pieces], axis=0)
                im = jnp.concatenate([piece[SHARE:] for piece in pieces], axis=0)
                rows = slice(p * PART, (p + 1) * PART)
                left[rows, g * LANES : (g + 1) * LANES] = re.astype(jnp.bfloat16)
                left[rows, bins + g * LANES : bins + (g + 1) * LANES] = im.astype(jnp.bfloat16)
        result = jnp.dot(left[...], inv[...], preferred_element_type=jnp.float32) * norm
        for p in range(SLOTS):
            out[p, half * PART : (half + 1) * PART, :] = result[p * PART : (p + 1) * PART]

    for half in range(2):
        final_wait(half).wait_send()


def body(traces, offsets, counts):
    segments, channels, length = traces.shape
    bins = length // 2
    norm = 1.0 / math.sqrt(bins * segments * WIN)
    rows = segments * PART
    bf16, f32 = jnp.bfloat16, jnp.float32
    pairs = SLOTS * ROW
    tile = (2 * SHARE, LANES)
    block = (segments,) + tile
    cut = (segments // CUTS,) + tile
    any_space, vmem = pl.BlockSpec(memory_space=pl.ANY), pl.BlockSpec(memory_space=pltpu.VMEM)
    dma = pltpu.SemaphoreType.DMA
    return pl.pallas_call(
        functools.partial(kernel, norm),
        out_shape=jax.ShapeDtypeStruct((SLOTS, channels // WIN, length), f32),
        in_specs=[any_space] * 5,
        out_specs=vmem,
        scratch_shapes=[
            pltpu.SMEM((SLOTS + 1, counts.shape[0]), jnp.int32),
            pltpu.VMEM((STEPS, segments, PART, length), bf16),
            pltpu.VMEM((length, length), bf16),
            pltpu.VMEM((bins, bins), bf16),
            pltpu.VMEM((length, length), bf16),
            pltpu.VMEM((8, bins), f32),
            pltpu.VMEM((rows, length), f32),
            pltpu.VMEM((rows, bins), bf16),
            pltpu.VMEM((rows, bins), bf16),
            pltpu.VMEM((rows, bins), f32),
            pltpu.VMEM((rows, LANES), f32),
            pltpu.VMEM((STEPS, CUTS, ROW) + cut, bf16),
            pltpu.VMEM((STEPS, CUTS, ROW + 2 * HALO) + cut, bf16),
            pltpu.VMEM((ROW + 2 * HALO,) + block, bf16),
            pltpu.VMEM((pairs,) + tile, f32),
            pltpu.VMEM((OUTSIDE, pairs) + tile, bf16),
            pltpu.VMEM((OUTSIDE, pairs) + tile, bf16),
            pltpu.VMEM((2, pairs) + tile, bf16),
            pltpu.VMEM((2, ROW, SLOTS) + tile, bf16),
            pltpu.VMEM((SLOTS * PART, length), bf16),
            dma((4,)),
            dma((STEPS,)),
            dma((STEPS, CUTS)),
            dma((STEPS, CUTS)),
            dma((STEPS, CUTS)),
            dma((STEPS, CUTS)),
            dma((OUTSIDE,)),
            dma((OUTSIDE,)),
            dma((2,)),
            dma((2,)),
        ],
        compiler_params=pltpu.CompilerParams(collective_id=0, has_side_effects=True, vmem_limit_bytes=VMEM_BYTES),
    )(
        jnp.concatenate([offsets.T, counts[None]]),
        traces,
        jnp.asarray(forward_table(length)),
        jnp.asarray(band_table(bins)),
        jnp.asarray(inverse_table(length)),
    )


def solution(mesh):
    in_specs = (P("win", "chan", None), P(), P())
    out_specs = P("chan", "win", None)
    return jax.shard_map(body, mesh=mesh, in_specs=in_specs, out_specs=out_specs, check_vma=False)
```

```python
import functools
import math

import jax
import jax.numpy as jnp
import numpy as np
from jax import lax
from jax.experimental import pallas as pl
from jax.experimental.pallas import tpu as pltpu
from jax.sharding import PartitionSpec as P

MESH = pl.DeviceIdType.MESH
RADIUS = 8
HALO = 3
SLOTS = 3
WATER = 0.8
EPS = 1e-06
ROW = 8
WIN = 8
PART = 16
SHARE = 8
LANES = 128
VMEM_BYTES = 107 << 19

ORDER = [(where, half) for where in (-4, 3, -3, 2, -2, 1, -1, 0) for half in (0, 1)]
STEPS = len(ORDER)
OUTSIDE = STEPS - 2
GREETED = [0, 1, 2, 0, 2, 0, 2, 1]
FARTHEST_FIRST = [4, 3, 5, 2, 6, 1, 7]
CUTS = 2
WINDOW = 3
LAG = 2


def forward_table(length):
    column = np.arange(length)
    phase = np.arange(length)[:, None] * (column % (length // 2))[None, :] % length
    angles = phase * (2.0 * math.pi / length)
    table = np.where(column[None, :] < length // 2, np.cos(angles), -np.sin(angles))
    return table.astype(jnp.bfloat16)


def inverse_table(length):
    column = np.arange(length)
    phase = np.arange(length)[None, :] * (column % (length // 2))[:, None] % length
    angles = phase * (2.0 * math.pi / length)
    table = np.where(column[:, None] < length // 2, np.cos(angles), -np.sin(angles))
    return table.astype(jnp.bfloat16)


def band_table(bins):
    place = np.arange(bins)
    return (np.abs(place[:, None] - place[None, :]) <= RADIUS).astype(jnp.bfloat16)


def arrival(step):
    where, half = ORDER[step]
    if where in (-4, 3):
        return -1
    return ORDER.index((where - 1 if where <= 0 else where + 1, half))


def entry_of(step, win):
    nearest = list(range(OUTSIDE - 4)) + [OUTSIDE - 2, OUTSIDE - 1, OUTSIDE - 4, OUTSIDE - 3, STEPS - 2, STEPS - 1]
    second = list(range(OUTSIDE - 8)) + [OUTSIDE - 6, OUTSIDE - 5, OUTSIDE - 8, OUTSIDE - 7]
    second += nearest[OUTSIDE - 4 :]
    place = jnp.where((win == 1) | (win == 4), look_up(step, nearest), step)
    return jnp.where(win == 2, look_up(step, second), place)


def look_up(step, values):
    found = jnp.int32(values[0])
    for k, value in enumerate(values[1:], 1):
        if value != values[0]:
            found = jnp.where(step == k, jnp.int32(value), found)
    return found


def kernel(
    norm, pairs_in, traces, forward, band, inverse, out,
    pairs, tr, fwd, bnd, inv, weight, spec, high, low, smooth, water, white, got, near, part, zout, zin,
    fout, fin, left, tab_sem, tr_sem, xs, xr, ys, yr, zs, zr, fs, fr,
):
    segments, bins = tr.shape[1], bnd.shape[0]
    groups = bins // LANES
    chan, win = lax.axis_index("chan"), lax.axis_index("win")
    row, place = chan // ROW, chan % ROW
    first = row * ROW
    above = lax.rem(row + 1, 4) * ROW + place
    below = lax.rem(row + 3, 4) * ROW + place
    after, before = lax.rem(win + 1, WIN), lax.rem(win + WIN - 1, WIN)

    barrier = pltpu.get_barrier_semaphore()
    mates = [(first + lax.rem(place + k, ROW), win) for k in FARTHEST_FIRST]
    partners = mates + [(above, win), (below, win)]
    beside = [(chan, after), (chan, before)]
    greeted = look_up(win, GREETED)
    for partner in partners:
        pl.semaphore_signal(barrier, inc=1, device_id=partner, device_id_type=MESH)

    def trace_copy(i):
        entry = entry_of(i, win)
        target = lax.rem(win + look_up(entry, [(where + WIN) % WIN for where, _ in ORDER]), WIN)
        half = look_up(entry, [half for _, half in ORDER])
        rows = pl.ds(pl.multiple_of((2 * target + half) * PART, PART), PART)
        return pltpu.make_async_copy(traces.at[:, rows, :], tr.at[i], tr_sem.at[i])

    tables = [
        pltpu.make_async_copy(source, target, tab_sem.at[k])
        for k, (source, target) in enumerate(
            [(forward, fwd), (band, bnd), (inverse, inv), (pairs_in, pairs)]
        )
    ]
    tables[0].start()
    trace_copy(0).start()
    tables[1].start()

    def start_traces(i, carry):
        trace_copy(i).start()
        return carry

    lax.fori_loop(1, STEPS, start_traces, 0)
    for table in tables[2:]:
        table.start()
    bin_of = lax.broadcasted_iota(jnp.int32, weight.shape, 1)
    count = jnp.minimum(bin_of + RADIUS, bins - 1) - jnp.maximum(bin_of - RADIUS, 0) + 1
    weight[...] = 1.0 / count.astype(jnp.float32)
    tables[0].wait()
    tables[1].wait()

    def whiten(i):
        trace_copy(i).wait()
        lhs = tr[i].reshape(segments * PART, 2 * bins)
        spec[...] = jnp.dot(lhs, fwd[...], preferred_element_type=jnp.float32)
        for s in range(segments):
            rows = slice(s * PART, (s + 1) * PART)
            re, im = spec[rows, :bins], spec[rows, bins:]
            amp = jnp.sqrt(re * re + im * im)
            top = amp.astype(jnp.bfloat16)
            high[rows, :] = top
            low[rows, :] = (amp - top.astype(jnp.float32)).astype(jnp.bfloat16)
            mean = jnp.sum(amp, axis=1, keepdims=True) * (1.0 / bins)
            water[rows, :] = jnp.broadcast_to(WATER * mean + EPS, (PART, LANES))
        smooth[...] = jnp.dot(high[...], bnd[...], preferred_element_type=jnp.float32) + jnp.dot(
            low[...], bnd[...], preferred_element_type=jnp.float32
        )
        for s in range(segments):
            rows = slice(s * PART, (s + 1) * PART)
            level = water[rows, :]
            for g in range(groups):
                lanes = slice(g * LANES, (g + 1) * LANES)
                scale = 1.0 / jnp.maximum(smooth[rows, lanes] * weight[0:1, lanes], level)
                re = spec[rows, lanes] * scale
                im = spec[rows, slice(bins + g * LANES, bins + (g + 1) * LANES)] * scale
                for h in range(2):
                    share = slice(h * SHARE, (h + 1) * SHARE)
                    both = jnp.concatenate([re[share], im[share]], axis=0)
                    white[i, s // (segments // CUTS), 2 * g + h, s % (segments // CUTS)] = both.astype(jnp.bfloat16)

    def send_row(i, c):
        for k, mate in enumerate(mates):
            other = lax.rem(place + FARTHEST_FIRST[k], ROW)
            pltpu.make_async_remote_copy(
                white.at[i, c, other],
                got.at[i, c, HALO + place],
                xs.at[i, c],
                xr.at[i, c],
                device_id=mate,
                device_id_type=MESH,
            ).start()

    def row_wait(i, c):
        block = got.at[i, c, pl.ds(0, ROW - 1)]
        return pltpu.make_async_remote_copy(
            block, block, xs.at[i, c], xr.at[i, c], device_id=mates[0], device_id_type=MESH
        )

    def near_copy(i, c, source, target, device):
        return pltpu.make_async_remote_copy(
            got.at[i, c, pl.ds(source, HALO)],
            got.at[i, c, pl.ds(target, HALO)],
            ys.at[i, c],
            yr.at[i, c],
            device_id=(device, win),
            device_id_type=MESH,
        )

    def near_wait(i, c):
        block = got.at[i, c, pl.ds(0, 2 * HALO)]
        return pltpu.make_async_remote_copy(
            block, block, ys.at[i, c], yr.at[i, c], device_id=(above, win), device_id_type=MESH
        )

    def chain_copy(i):
        forth = look_up(i, [int(where > 0) for where, _ in ORDER])
        target = jnp.where(forth == 1, after, before)
        return pltpu.make_async_remote_copy(
            zout.at[i], zin.at[i], zs.at[i], zr.at[i], device_id=(chan, target), device_id_type=MESH
        )

    def cross(i):
        def move(b, carry):
            for c in range(CUTS):
                near[b, pl.ds(c * (segments // CUTS), segments // CUTS)] = got[i, c, b]
            return carry

        lax.fori_loop(0, ROW + 2 * HALO, move, 0, unroll=True)

        def owner(j, carry):
            source = [near[HALO + j, s].astype(jnp.float32) for s in range(segments)]
            for p in range(SLOTS):
                receiver = HALO + j + pairs[p, first + j]
                live = p < pairs[SLOTS, first + j]
                total_re = jnp.zeros((SHARE, LANES), jnp.float32)
                total_im = jnp.zeros((SHARE, LANES), jnp.float32)
                for s, both in enumerate(source):
                    ar, ai = both[:SHARE], both[SHARE:]
                    other = near[receiver, s].astype(jnp.float32)
                    br, bi = other[:SHARE], other[SHARE:]
                    total_re += ar * br + ai * bi
                    total_im += ar * bi - ai * br
                total = jnp.concatenate([total_re, total_im], axis=0)
                part[SLOTS * j + p] = jnp.where(live, total, 0.0)
            return carry

        lax.fori_loop(0, ROW, owner, 0, unroll=2)

    def add_up(i):
        slot = look_up(i, [max(arrival(step), 0) for step in range(STEPS)])
        joins = look_up(i, [int(arrival(step) >= 0) for step in range(STEPS)]) == 1

        @pl.when(jnp.logical_not(joins))
        def _():
            zout[i] = part[...].astype(jnp.bfloat16)
            chain_copy(i).start()

        @pl.when(joins & (i < OUTSIDE))
        def _():
            chain_copy(slot).wait_recv()
            zout[i] = (part[...] + zin[slot].astype(jnp.float32)).astype(jnp.bfloat16)
            chain_copy(i).start()

        @pl.when(i >= OUTSIDE)
        def _():
            half = i - OUTSIDE
            chain_copy(slot).wait_recv()
            chain_copy(slot - 2).wait_recv()
            total = part[...] + zin[slot].astype(jnp.float32) + zin[slot - 2].astype(jnp.float32)
            fout[half] = total.astype(jnp.bfloat16)
            for k, mate in enumerate(mates):
                other = lax.rem(place + FARTHEST_FIRST[k], ROW)
                pltpu.make_async_remote_copy(
                    fout.at[half, pl.ds(SLOTS * other, SLOTS)],
                    fin.at[half, place],
                    fs.at[half],
                    fr.at[half],
                    device_id=mate,
                    device_id_type=MESH,
                ).start()
            fin[half, place] = fout[half, pl.ds(SLOTS * place, SLOTS)]

    def final_wait(half):
        block = fin.at[half, pl.ds(0, ROW - 1)]
        return pltpu.make_async_remote_copy(
            block, block, fs.at[half], fr.at[half], device_id=mates[0], device_id_type=MESH
        )

    def step(n, carry):
        send, arrived, paired = n - 1, n - 1 - WINDOW, n - 1 - WINDOW - LAG

        @pl.when(send == 0)
        def _():
            pl.semaphore_wait(barrier, len(partners) + greeted)
            for partner in beside:
                pl.semaphore_signal(barrier, inc=1, device_id=partner, device_id_type=MESH)

        @pl.when((arrived >= 0) & (arrived < STEPS))
        def _():
            for c in range(CUTS):
                row_wait(arrived, c).wait_recv()
                near_copy(arrived, c, HALO, HALO + ROW, below).start()
                near_copy(arrived, c, ROW, 0, above).start()

        @pl.when((send >= 0) & (send < STEPS))
        def _():
            for c in range(CUTS):
                send_row(send, c)
            for c in range(CUTS):
                got[send, c, HALO + place] = white[send, c, place]

        @pl.when(n < STEPS)
        def _():
            whiten(n)

        @pl.when(paired == 0)
        def _():
            tables[3].wait()

            @pl.when(greeted < len(beside))
            def _():
                pl.semaphore_wait(barrier, len(beside) - greeted)

        @pl.when(paired >= 0)
        def _():
            for c in range(CUTS):
                near_wait(paired, c).wait_recv()
            cross(paired)
            add_up(entry_of(paired, win))

        return carry

    lax.fori_loop(0, STEPS + 1 + WINDOW + LAG, step, 0)

    def drain(i, carry):
        for c in range(CUTS):
            row_wait(i, c).wait_send()
            near_wait(i, c).wait_send()

        @pl.when(i < OUTSIDE)
        def _():
            chain_copy(i).wait_send()

        return carry

    lax.fori_loop(0, STEPS, drain, 0)

    tables[2].wait()
    for half in range(2):
        final_wait(half).wait_recv()
        for g in range(groups):
            for p in range(SLOTS):
                pieces = [fin[half, 2 * g + h, p].astype(jnp.float32) for h in range(2)]
                re = jnp.concatenate([piece[:SHARE] for piece in pieces], axis=0)
                im = jnp.concatenate([piece[SHARE:] for piece in pieces], axis=0)
                rows = slice(p * PART, (p + 1) * PART)
                left[rows, g * LANES : (g + 1) * LANES] = re.astype(jnp.bfloat16)
                left[rows, bins + g * LANES : bins + (g + 1) * LANES] = im.astype(jnp.bfloat16)
        result = jnp.dot(left[...], inv[...], preferred_element_type=jnp.float32) * norm
        for p in range(SLOTS):
            out[p, half * PART : (half + 1) * PART, :] = result[p * PART : (p + 1) * PART]

    for half in range(2):
        final_wait(half).wait_send()


def body(traces, offsets, counts):
    segments, channels, length = traces.shape
    bins = length // 2
    norm = 1.0 / math.sqrt(bins * segments * WIN)
    rows = segments * PART
    bf16, f32 = jnp.bfloat16, jnp.float32
    pairs = SLOTS * ROW
    tile = (2 * SHARE, LANES)
    block = (segments,) + tile
    cut = (segments // CUTS,) + tile
    any_space, vmem = pl.BlockSpec(memory_space=pl.ANY), pl.BlockSpec(memory_space=pltpu.VMEM)
    dma = pltpu.SemaphoreType.DMA
    return pl.pallas_call(
        functools.partial(kernel, norm),
        out_shape=jax.ShapeDtypeStruct((SLOTS, channels // WIN, length), f32),
        in_specs=[any_space] * 5,
        out_specs=vmem,
        scratch_shapes=[
            pltpu.SMEM((SLOTS + 1, counts.shape[0]), jnp.int32),
            pltpu.VMEM((STEPS, segments, PART, length), bf16),
            pltpu.VMEM((length, length), bf16),
            pltpu.VMEM((bins, bins), bf16),
            pltpu.VMEM((length, length), bf16),
            pltpu.VMEM((8, bins), f32),
            pltpu.VMEM((rows, length), f32),
            pltpu.VMEM((rows, bins), bf16),
            pltpu.VMEM((rows, bins), bf16),
            pltpu.VMEM((rows, bins), f32),
            pltpu.VMEM((rows, LANES), f32),
            pltpu.VMEM((STEPS, CUTS, ROW) + cut, bf16),
            pltpu.VMEM((STEPS, CUTS, ROW + 2 * HALO) + cut, bf16),
            pltpu.VMEM((ROW + 2 * HALO,) + block, bf16),
            pltpu.VMEM((pairs,) + tile, f32),
            pltpu.VMEM((OUTSIDE, pairs) + tile, bf16),
            pltpu.VMEM((OUTSIDE, pairs) + tile, bf16),
            pltpu.VMEM((2, pairs) + tile, bf16),
            pltpu.VMEM((2, ROW, SLOTS) + tile, bf16),
            pltpu.VMEM((SLOTS * PART, length), bf16),
            dma((4,)),
            dma((STEPS,)),
            dma((STEPS, CUTS)),
            dma((STEPS, CUTS)),
            dma((STEPS, CUTS)),
            dma((STEPS, CUTS)),
            dma((OUTSIDE,)),
            dma((OUTSIDE,)),
            dma((2,)),
            dma((2,)),
        ],
        compiler_params=pltpu.CompilerParams(collective_id=0, has_side_effects=True, vmem_limit_bytes=VMEM_BYTES),
    )(
        jnp.concatenate([offsets.T, counts[None]]),
        traces,
        jnp.asarray(forward_table(length)),
        jnp.asarray(band_table(bins)),
        jnp.asarray(inverse_table(length)),
    )


def solution(mesh):
    in_specs = (P("win", "chan", None), P(), P())
    out_specs = P("chan", "win", None)
    return jax.shard_map(body, mesh=mesh, in_specs=in_specs, out_specs=out_specs, check_vma=False)
```

```python
import functools
import math

import jax
import jax.numpy as jnp
import numpy as np
from jax import lax
from jax.experimental import pallas as pl
from jax.experimental.pallas import tpu as pltpu
from jax.sharding import PartitionSpec as P

MESH = pl.DeviceIdType.MESH
RADIUS = 8
HALO = 3
SLOTS = 3
WATER = 0.8
EPS = 1e-06
ROW = 8
WIN = 8
PART = 16
SHARE = 8
LANES = 128
VMEM_BYTES = 107 << 19

ORDER = [(where, half) for where in (-4, 3, -3, 2, -2, 1, -1, 0) for half in (0, 1)]
STEPS = len(ORDER)
OUTSIDE = STEPS - 2
GREETED = [0, 1, 2, 0, 2, 0, 2, 1]
FARTHEST_FIRST = [4, 3, 5, 2, 6, 1, 7]
CUTS = 2
WINDOW = 3
LAG = 2


def forward_table(length):
    column = np.arange(length)
    phase = np.arange(length)[:, None] * (column % (length // 2))[None, :] % length
    angles = phase * (2.0 * math.pi / length)
    table = np.where(column[None, :] < length // 2, np.cos(angles), -np.sin(angles))
    return table.astype(jnp.bfloat16)


def inverse_table(length):
    column = np.arange(length)
    phase = np.arange(length)[None, :] * (column % (length // 2))[:, None] % length
    angles = phase * (2.0 * math.pi / length)
    table = np.where(column[:, None] < length // 2, np.cos(angles), -np.sin(angles))
    return table.astype(jnp.bfloat16)


def band_table(bins):
    place = np.arange(bins)
    return (np.abs(place[:, None] - place[None, :]) <= RADIUS).astype(jnp.bfloat16)


def arrival(step):
    where, half = ORDER[step]
    if where in (-4, 3):
        return -1
    return ORDER.index((where - 1 if where <= 0 else where + 1, half))


def entry_of(step, win):
    nearest = list(range(OUTSIDE - 4)) + [OUTSIDE - 2, OUTSIDE - 1, OUTSIDE - 4, OUTSIDE - 3, STEPS - 2, STEPS - 1]
    second = list(range(OUTSIDE - 8)) + [OUTSIDE - 6, OUTSIDE - 5, OUTSIDE - 8, OUTSIDE - 7]
    second += nearest[OUTSIDE - 4 :]
    place = jnp.where((win == 1) | (win == 4), look_up(step, nearest), step)
    last = list(range(OUTSIDE - 6)) + [OUTSIDE - 4, OUTSIDE - 3, OUTSIDE - 6, OUTSIDE - 5] + list(range(OUTSIDE - 2, STEPS))
    place = jnp.where(win == 7, look_up(step, last), place)
    return jnp.where(win == 2, look_up(step, second), place)


def look_up(step, values):
    found = jnp.int32(values[0])
    for k, value in enumerate(values[1:], 1):
        if value != values[0]:
            found = jnp.where(step == k, jnp.int32(value), found)
    return found


def kernel(
    norm, pairs_in, traces, forward, band, inverse, out,
    pairs, tr, fwd, bnd, inv, weight, spec, high, low, smooth, water, white, got, near, part, zout, zin,
    fout, fin, left, tab_sem, tr_sem, xs, xr, ys, yr, zs, zr, fs, fr,
):
    segments, bins = tr.shape[1], bnd.shape[0]
    groups = bins // LANES
    chan, win = lax.axis_index("chan"), lax.axis_index("win")
    row, place = chan // ROW, chan % ROW
    first = row * ROW
    above = lax.rem(row + 1, 4) * ROW + place
    below = lax.rem(row + 3, 4) * ROW + place
    after, before = lax.rem(win + 1, WIN), lax.rem(win + WIN - 1, WIN)

    barrier = pltpu.get_barrier_semaphore()
    mates = [(first + lax.rem(place + k, ROW), win) for k in FARTHEST_FIRST]
    partners = mates + [(above, win), (below, win)]
    beside = [(chan, after), (chan, before)]
    greeted = look_up(win, GREETED)
    for partner in partners:
        pl.semaphore_signal(barrier, inc=1, device_id=partner, device_id_type=MESH)

    def trace_copy(i):
        entry = entry_of(i, win)
        target = lax.rem(win + look_up(entry, [(where + WIN) % WIN for where, _ in ORDER]), WIN)
        half = look_up(entry, [half for _, half in ORDER])
        rows = pl.ds(pl.multiple_of((2 * target + half) * PART, PART), PART)
        return pltpu.make_async_copy(traces.at[:, rows, :], tr.at[i], tr_sem.at[i])

    tables = [
        pltpu.make_async_copy(source, target, tab_sem.at[k])
        for k, (source, target) in enumerate(
            [(forward, fwd), (band, bnd), (inverse, inv), (pairs_in, pairs)]
        )
    ]
    tables[0].start()
    trace_copy(0).start()
    tables[1].start()

    def start_traces(i, carry):
        trace_copy(i).start()
        return carry

    lax.fori_loop(1, STEPS, start_traces, 0)
    for table in tables[2:]:
        table.start()
    bin_of = lax.broadcasted_iota(jnp.int32, weight.shape, 1)
    count = jnp.minimum(bin_of + RADIUS, bins - 1) - jnp.maximum(bin_of - RADIUS, 0) + 1
    weight[...] = 1.0 / count.astype(jnp.float32)
    tables[0].wait()
    tables[1].wait()

    def whiten(i):
        trace_copy(i).wait()
        lhs = tr[i].reshape(segments * PART, 2 * bins)
        spec[...] = jnp.dot(lhs, fwd[...], preferred_element_type=jnp.float32)
        for s in range(segments):
            rows = slice(s * PART, (s + 1) * PART)
            re, im = spec[rows, :bins], spec[rows, bins:]
            amp = jnp.sqrt(re * re + im * im)
            top = amp.astype(jnp.bfloat16)
            high[rows, :] = top
            low[rows, :] = (amp - top.astype(jnp.float32)).astype(jnp.bfloat16)
            mean = jnp.sum(amp, axis=1, keepdims=True) * (1.0 / bins)
            water[rows, :] = jnp.broadcast_to(WATER * mean + EPS, (PART, LANES))
        smooth[...] = jnp.dot(high[...], bnd[...], preferred_element_type=jnp.float32) + jnp.dot(
            low[...], bnd[...], preferred_element_type=jnp.float32
        )
        for s in range(segments):
            rows = slice(s * PART, (s + 1) * PART)
            level = water[rows, :]
            for g in range(groups):
                lanes = slice(g * LANES, (g + 1) * LANES)
                scale = 1.0 / jnp.maximum(smooth[rows, lanes] * weight[0:1, lanes], level)
                re = spec[rows, lanes] * scale
                im = spec[rows, slice(bins + g * LANES, bins + (g + 1) * LANES)] * scale
                for h in range(2):
                    share = slice(h * SHARE, (h + 1) * SHARE)
                    both = jnp.concatenate([re[share], im[share]], axis=0)
                    white[i, s // (segments // CUTS), 2 * g + h, s % (segments // CUTS)] = both.astype(jnp.bfloat16)

    def send_row(i, c):
        for k, mate in enumerate(mates):
            other = lax.rem(place + FARTHEST_FIRST[k], ROW)
            pltpu.make_async_remote_copy(
                white.at[i, c, other],
                got.at[i, c, HALO + place],
                xs.at[i, c],
                xr.at[i, c],
                device_id=mate,
                device_id_type=MESH,
            ).start()

    def row_wait(i, c):
        block = got.at[i, c, pl.ds(0, ROW - 1)]
        return pltpu.make_async_remote_copy(
            block, block, xs.at[i, c], xr.at[i, c], device_id=mates[0], device_id_type=MESH
        )

    def near_copy(i, c, source, target, device):
        return pltpu.make_async_remote_copy(
            got.at[i, c, pl.ds(source, HALO)],
            got.at[i, c, pl.ds(target, HALO)],
            ys.at[i, c],
            yr.at[i, c],
            device_id=(device, win),
            device_id_type=MESH,
        )

    def near_wait(i, c):
        block = got.at[i, c, pl.ds(0, 2 * HALO)]
        return pltpu.make_async_remote_copy(
            block, block, ys.at[i, c], yr.at[i, c], device_id=(above, win), device_id_type=MESH
        )

    def chain_copy(i):
        forth = look_up(i, [int(where > 0) for where, _ in ORDER])
        target = jnp.where(forth == 1, after, before)
        return pltpu.make_async_remote_copy(
            zout.at[i], zin.at[i], zs.at[i], zr.at[i], device_id=(chan, target), device_id_type=MESH
        )

    def cross(i):
        def move(b, carry):
            for c in range(CUTS):
                near[b, pl.ds(c * (segments // CUTS), segments // CUTS)] = got[i, c, b]
            return carry

        lax.fori_loop(0, ROW + 2 * HALO, move, 0, unroll=True)

        def owner(j, carry):
            source = [near[HALO + j, s].astype(jnp.float32) for s in range(segments)]
            for p in range(SLOTS):
                receiver = HALO + j + pairs[p, first + j]
                live = p < pairs[SLOTS, first + j]
                total_re = jnp.zeros((SHARE, LANES), jnp.float32)
                total_im = jnp.zeros((SHARE, LANES), jnp.float32)
                for s, both in enumerate(source):
                    ar, ai = both[:SHARE], both[SHARE:]
                    other = near[receiver, s].astype(jnp.float32)
                    br, bi = other[:SHARE], other[SHARE:]
                    total_re += ar * br + ai * bi
                    total_im += ar * bi - ai * br
                total = jnp.concatenate([total_re, total_im], axis=0)
                part[SLOTS * j + p] = jnp.where(live, total, 0.0)
            return carry

        lax.fori_loop(0, ROW, owner, 0, unroll=2)

    def add_up(i):
        slot = look_up(i, [max(arrival(step), 0) for step in range(STEPS)])
        joins = look_up(i, [int(arrival(step) >= 0) for step in range(STEPS)]) == 1

        @pl.when(jnp.logical_not(joins))
        def _():
            zout[i] = part[...].astype(jnp.bfloat16)
            chain_copy(i).start()

        @pl.when(joins & (i < OUTSIDE))
        def _():
            chain_copy(slot).wait_recv()
            zout[i] = (part[...] + zin[slot].astype(jnp.float32)).astype(jnp.bfloat16)
            chain_copy(i).start()

        @pl.when(i >= OUTSIDE)
        def _():
            half = i - OUTSIDE
            chain_copy(slot).wait_recv()
            chain_copy(slot - 2).wait_recv()
            total = part[...] + zin[slot].astype(jnp.float32) + zin[slot - 2].astype(jnp.float32)
            fout[half] = total.astype(jnp.bfloat16)
            for k, mate in enumerate(mates):
                other = lax.rem(place + FARTHEST_FIRST[k], ROW)
                pltpu.make_async_remote_copy(
                    fout.at[half, pl.ds(SLOTS * other, SLOTS)],
                    fin.at[half, place],
                    fs.at[half],
                    fr.at[half],
                    device_id=mate,
                    device_id_type=MESH,
                ).start()
            fin[half, place] = fout[half, pl.ds(SLOTS * place, SLOTS)]

    def final_wait(half):
        block = fin.at[half, pl.ds(0, ROW - 1)]
        return pltpu.make_async_remote_copy(
            block, block, fs.at[half], fr.at[half], device_id=mates[0], device_id_type=MESH
        )

    def step(n, carry):
        send, arrived, paired = n - 1, n - 1 - WINDOW, n - 1 - WINDOW - LAG

        @pl.when(send == 0)
        def _():
            pl.semaphore_wait(barrier, len(partners) + greeted)
            for partner in beside:
                pl.semaphore_signal(barrier, inc=1, device_id=partner, device_id_type=MESH)

        @pl.when((arrived >= 0) & (arrived < STEPS))
        def _():
            for c in range(CUTS):
                row_wait(arrived, c).wait_recv()
                near_copy(arrived, c, HALO, HALO + ROW, below).start()
                near_copy(arrived, c, ROW, 0, above).start()

        @pl.when((send >= 0) & (send < STEPS))
        def _():
            for c in range(CUTS):
                send_row(send, c)
            for c in range(CUTS):
                got[send, c, HALO + place] = white[send, c, place]

        @pl.when(n < STEPS)
        def _():
            whiten(n)

        @pl.when(paired == 0)
        def _():
            tables[3].wait()

            @pl.when(greeted < len(beside))
            def _():
                pl.semaphore_wait(barrier, len(beside) - greeted)

        @pl.when(paired >= 0)
        def _():
            for c in range(CUTS):
                near_wait(paired, c).wait_recv()
            cross(paired)
            add_up(entry_of(paired, win))

        return carry

    lax.fori_loop(0, STEPS + 1 + WINDOW + LAG, step, 0)

    def drain(i, carry):
        for c in range(CUTS):
            row_wait(i, c).wait_send()
            near_wait(i, c).wait_send()

        @pl.when(i < OUTSIDE)
        def _():
            chain_copy(i).wait_send()

        return carry

    lax.fori_loop(0, STEPS, drain, 0)

    tables[2].wait()
    for half in range(2):
        final_wait(half).wait_recv()
        for g in range(groups):
            for p in range(SLOTS):
                pieces = [fin[half, 2 * g + h, p].astype(jnp.float32) for h in range(2)]
                re = jnp.concatenate([piece[:SHARE] for piece in pieces], axis=0)
                im = jnp.concatenate([piece[SHARE:] for piece in pieces], axis=0)
                rows = slice(p * PART, (p + 1) * PART)
                left[rows, g * LANES : (g + 1) * LANES] = re.astype(jnp.bfloat16)
                left[rows, bins + g * LANES : bins + (g + 1) * LANES] = im.astype(jnp.bfloat16)
        result = jnp.dot(left[...], inv[...], preferred_element_type=jnp.float32) * norm
        for p in range(SLOTS):
            out[p, half * PART : (half + 1) * PART, :] = result[p * PART : (p + 1) * PART]

    for half in range(2):
        final_wait(half).wait_send()


def body(traces, offsets, counts):
    segments, channels, length = traces.shape
    bins = length // 2
    norm = 1.0 / math.sqrt(bins * segments * WIN)
    rows = segments * PART
    bf16, f32 = jnp.bfloat16, jnp.float32
    pairs = SLOTS * ROW
    tile = (2 * SHARE, LANES)
    block = (segments,) + tile
    cut = (segments // CUTS,) + tile
    any_space, vmem = pl.BlockSpec(memory_space=pl.ANY), pl.BlockSpec(memory_space=pltpu.VMEM)
    dma = pltpu.SemaphoreType.DMA
    return pl.pallas_call(
        functools.partial(kernel, norm),
        out_shape=jax.ShapeDtypeStruct((SLOTS, channels // WIN, length), f32),
        in_specs=[any_space] * 5,
        out_specs=vmem,
        scratch_shapes=[
            pltpu.SMEM((SLOTS + 1, counts.shape[0]), jnp.int32),
            pltpu.VMEM((STEPS, segments, PART, length), bf16),
            pltpu.VMEM((length, length), bf16),
            pltpu.VMEM((bins, bins), bf16),
            pltpu.VMEM((length, length), bf16),
            pltpu.VMEM((8, bins), f32),
            pltpu.VMEM((rows, length), f32),
            pltpu.VMEM((rows, bins), bf16),
            pltpu.VMEM((rows, bins), bf16),
            pltpu.VMEM((rows, bins), f32),
            pltpu.VMEM((rows, LANES), f32),
            pltpu.VMEM((STEPS, CUTS, ROW) + cut, bf16),
            pltpu.VMEM((STEPS, CUTS, ROW + 2 * HALO) + cut, bf16),
            pltpu.VMEM((ROW + 2 * HALO,) + block, bf16),
            pltpu.VMEM((pairs,) + tile, f32),
            pltpu.VMEM((OUTSIDE, pairs) + tile, bf16),
            pltpu.VMEM((OUTSIDE, pairs) + tile, bf16),
            pltpu.VMEM((2, pairs) + tile, bf16),
            pltpu.VMEM((2, ROW, SLOTS) + tile, bf16),
            pltpu.VMEM((SLOTS * PART, length), bf16),
            dma((4,)),
            dma((STEPS,)),
            dma((STEPS, CUTS)),
            dma((STEPS, CUTS)),
            dma((STEPS, CUTS)),
            dma((STEPS, CUTS)),
            dma((OUTSIDE,)),
            dma((OUTSIDE,)),
            dma((2,)),
            dma((2,)),
        ],
        compiler_params=pltpu.CompilerParams(collective_id=0, has_side_effects=True, vmem_limit_bytes=VMEM_BYTES),
    )(
        jnp.concatenate([offsets.T, counts[None]]),
        traces,
        jnp.asarray(forward_table(length)),
        jnp.asarray(band_table(bins)),
        jnp.asarray(inverse_table(length)),
    )


def solution(mesh):
    in_specs = (P("win", "chan", None), P(), P())
    out_specs = P("chan", "win", None)
    return jax.shard_map(body, mesh=mesh, in_specs=in_specs, out_specs=out_specs, check_vma=False)
```
